128 devices in a mesh: visit: 8 (over y_lo, z), patch: 16 (over y_hi, x, core).
Axes of the slice: x: 4, y: 4 (y_hi: 2, y_lo: 2; y = y_hi * 2 + y_lo), z: 4, core: 2. Of those that a mesh axis runs over, the one named last changes fastest.
Arguments:
- pixels: bfloat16 [16, 16, 4, 512, 512], P('patch', 'visit'), may hold values from -6 to 6
- row_mask: int32 [16, 16, 4, 512], P('patch', 'visit'), may hold values 0 or 1
- col_mask: int32 [16, 16, 4, 512], P('patch', 'visit'), may hold values 0 or 1
- route: int32 [16, 16, 4], P('patch', 'visit'), may hold values from 0 to 15, as said below
- tile: int32 [16, 16, 4], P('patch', 'visit'), may hold values from 0 to 3
- wcs_offset: int32 [16, 16, 4, 2], P('patch', 'visit'), may hold values from -8 to 8
- subpixel: bfloat16 [16, 16, 4, 2], P('patch', 'visit'), may hold values from 0 to 1
- plate_scale: bfloat16 [16, 16, 4], P('patch', 'visit'), may hold values from 0.9765625 to 1.015625
- stretch_weight: bfloat16 [16, 16, 4], P('patch', 'visit'), may hold values from 0.25 to 4
- psf_taps: float32 [16, 2, 41], P('visit'), may hold values from 0.05 to 1
Outputs:
- coadd_flux: float32 [1024, 16384], P('visit', 'patch')
- coadd_weight: float32 [1024, 16384], P('visit', 'patch')
- hessian: float32 [16, 10, 10], P('patch')
The draws below stay inside these ranges and needn't reach their ends.
Inputs may be any that keep to these rules, and one draw needn't show every extreme that they name: `route`: among the stretches of one CCD in one aligned block of 2 visits, at most 2 go to one patch; in every draw one patch receives exactly 2 stretches from every such block.
All inputs are finite; a program needn't handle non-finite values. No bound on the sum of `row_mask` or of `col_mask` on one device may be relied on, other than what follows from the above.
Results may differ from the reference program's by a relative error of at most 0.013.
Values may be sent and summed in bfloat16 or wider, within the bound.
A program may use at most 192 MiB of HBM per device.

```python
import math
import jax
import jax.numpy as jnp
import numpy as np
from jax import lax

S = 512
STRETCHES_CCD = 4
TILES = 4
TAPS = 41
VIS_DEV = 2
VISITS = 16
PATCHES = 16
CCDS = 16
CAP = 2


def draw_route(key, part):
    block_total = CCDS * (VISITS // VIS_DEV)
    per_block = VIS_DEV * STRETCHES_CCD
    hot_key, list_key = jax.random.split(key, 2)
    hottest = jax.random.randint(hot_key, (), 0, PATCHES)
    spares = (hottest + 1 + jnp.arange(PATCHES - 1)) % PATCHES
    spare_pool = jnp.tile(spares, CAP)
    pool_size = spare_pool.shape[0]

    def one_block(block_key):
        first_key, second_key = jax.random.split(block_key)
        first_scores = jax.random.randint(first_key, (pool_size,), 0, 1 << 16) * pool_size + jnp.arange(pool_size)
        chosen = spare_pool[jnp.argsort(first_scores, stable=True)][:per_block - CAP]
        filled = jnp.concatenate([chosen, jnp.full((CAP,), hottest)])
        second_scores = jax.random.randint(second_key, (per_block,), 0, 1 << 16) * per_block + jnp.arange(per_block)
        return filled[jnp.argsort(second_scores, stable=True)]
    block_keys = jax.random.split(list_key, block_total)
    routes = jax.vmap(one_block)(block_keys)
    return routes.reshape(CCDS, VISITS, STRETCHES_CCD).astype(jnp.int32)


def with_ends(values, rng, smallest, largest):
    index_at = [jax.random.randint(jax.random.fold_in(rng, axis), (), 0, length) for axis, length in enumerate(values.shape)]
    main_axis = values.shape.index(max(values.shape))
    neighbour = index_at[:main_axis] + [(index_at[main_axis] + 1) % values.shape[main_axis]] + index_at[main_axis + 1:]
    return values.at[tuple(index_at)].set(smallest).at[tuple(neighbour)].set(largest)


def block_scale(key, dims, cuts, smallest, high):
    def one(axis_at, blocks):
        heights = jax.random.uniform(jax.random.fold_in(jax.random.fold_in(key, 6), axis_at), (blocks,), jnp.float32, smallest / len(cuts), high / len(cuts))
        return jnp.repeat(jnp.exp(heights), dims[axis_at] // blocks).reshape((-1,) + (1,) * (len(dims) - axis_at - 1))

    factor_of = one(*cuts[0])
    for cut in cuts[1:]:
        factor_of = factor_of * one(*cut)
    return factor_of


def centred(own_key, dims, deviation, limit, cuts=(), kind=jnp.bfloat16):
    entries = jax.random.normal(own_key, dims, jnp.float32) * deviation
    if len(cuts) > 0:
        entries = block_scale(own_key, dims, cuts, -0.22, 0.18) * entries
    return jnp.clip(entries, min=-limit, max=limit).astype(kind)


def setup_inputs(seed: int = 0) -> dict:
    keys = jax.random.split(jax.random.key(seed), 11)
    return {
        "pixels": centred(keys[0], (CCDS, VISITS, STRETCHES_CCD, S, S), 1.0, 6.0, ((0, 16), (1, 8))),
        "row_mask": with_ends((jax.random.randint(keys[1], (CCDS, VISITS, STRETCHES_CCD, S), 0, 16) < 15).astype(jnp.int32), jax.random.fold_in(keys[1], 1), 0, 1),
        "col_mask": with_ends((jax.random.randint(keys[2], (CCDS, VISITS, STRETCHES_CCD, S), 0, 16) < 15).astype(jnp.int32), jax.random.fold_in(keys[2], 1), 0, 1),
        "route": draw_route(jax.random.fold_in(keys[10], 71), 0),
        "tile": with_ends(jax.random.randint(keys[4], (CCDS, VISITS, STRETCHES_CCD), 0, TILES), jax.random.fold_in(keys[4], 1), 0, TILES - 1).astype(jnp.int32),
        "wcs_offset": with_ends(jax.random.randint(keys[5], (CCDS, VISITS, STRETCHES_CCD, 2), -8, 9), jax.random.fold_in(keys[5], 1), -8, 8).astype(jnp.int32),
        "subpixel": jnp.clip(1.0 * jax.random.uniform(keys[6], (CCDS, VISITS, STRETCHES_CCD, 2), jnp.float32) ** block_scale(keys[6], (CCDS, VISITS, STRETCHES_CCD, 2), ((0, 16), (1, 8)), -0.2, 0.2), 0.0, 1.0).astype(jnp.bfloat16),
        "plate_scale": jnp.clip(0.9765625 + 0.0390625 * jax.random.uniform(keys[7], (CCDS, VISITS, STRETCHES_CCD), jnp.float32) ** block_scale(keys[7], (CCDS, VISITS, STRETCHES_CCD), ((0, 16), (1, 8)), -0.2, 0.2), 0.9765625, 1.015625).astype(jnp.bfloat16),
        "stretch_weight": jnp.clip(jnp.exp(math.log(4.0) - 2.7725887 * jax.random.uniform(keys[8], (CCDS, VISITS, STRETCHES_CCD), jnp.float32) ** block_scale(keys[8], (CCDS, VISITS, STRETCHES_CCD), ((0, 16), (1, 8)), -0.2, 0.2)), 0.25, 4.0).astype(jnp.bfloat16),
        "psf_taps": jnp.clip(jnp.exp(math.log(1.0) - 2.9957323 * jax.random.uniform(keys[9], (VISITS, 2, TAPS), jnp.float32) ** block_scale(keys[9], (VISITS, 2, TAPS), ((0, 8),), -0.2, 0.2)), 0.05, 1.0),
    }


PAIRS = ((0, 0), (1, 0), (0, 1), (2, 0), (1, 1), (0, 2), (3, 0), (2, 1), (1, 2), (0, 3))
precise = lax.Precision.HIGHEST


def pick_tables():
    row_pick = []
    col_pick = []
    for first in range(10):
        row_line = []
        col_line = []
        for second in range(10):
            row_line.append(PAIRS[first][0] * 4 + PAIRS[second][0])
            col_line.append(PAIRS[first][1] * 4 + PAIRS[second][1])
        row_pick.append(row_line)
        col_pick.append(col_line)
    return np.array(row_pick), np.array(col_pick)


def lanczos(offset):
    inside = jnp.abs(offset) < 3.0
    return jnp.where(inside, jnp.sinc(offset) * jnp.sinc(offset / 3.0), jnp.zeros_like(offset))


def source_positions(plate_factor, whole_shift, fraction, extent):
    grid_pos = jnp.arange(extent).astype(plate_factor.dtype)
    middle = extent / 2.0
    return plate_factor * (grid_pos - middle) + (middle + (whole_shift.astype(plate_factor.dtype) + fraction))


def legendre(coord):
    square = coord * coord
    return jnp.stack([jnp.ones_like(coord), coord, 1.5 * square - 0.5, (2.5 * square - 1.5) * coord])


def band_weights(source, extent, gain_value):
    lowest = jnp.floor(source) - 2.0
    tap_steps = jnp.arange(6).astype(source.dtype)
    spot_pos = lowest[:, None] + tap_steps[None, :]
    spot_index = spot_pos.astype(jnp.int32)
    inside_stretch = (spot_index >= 0) & (spot_index < extent)
    weights = (gain_value * lanczos(spot_pos - source[:, None])).astype(jnp.bfloat16)
    weights = jnp.where(inside_stretch, weights, jnp.zeros_like(weights))
    return jnp.clip(spot_index, 0, extent - 1), weights


def warp_stretch(cleaned, plate_factor, whole_shift, fraction, gain_value, rows_ok, cols_ok):
    extent = cleaned.shape[0]
    source_y = source_positions(plate_factor, whole_shift[0], fraction[0], extent)
    source_x = source_positions(plate_factor, whole_shift[1], fraction[1], extent)
    index_y, weight_y = band_weights(source_y, extent, 1.0)
    index_x, weight_x = band_weights(source_x, extent, gain_value)
    row_taps = cleaned[index_y].astype(jnp.float32)
    half_warp = jnp.sum(weight_y.astype(jnp.float32)[:, :, None] * row_taps, axis=1).astype(jnp.bfloat16)
    col_taps = half_warp[:, index_x].astype(jnp.float32)
    warped = jnp.sum(weight_x.astype(jnp.float32)[None, :, :] * col_taps, axis=2).astype(jnp.bfloat16)
    row_cover = jnp.sum(weight_y.astype(jnp.float32) * rows_ok.astype(jnp.float32)[index_y], axis=1).astype(jnp.bfloat16)
    col_cover = jnp.sum(weight_x.astype(jnp.float32) * cols_ok.astype(jnp.float32)[index_x], axis=1).astype(jnp.bfloat16)
    return warped, row_cover, col_cover


def stretch_moments(cleaned, row_block, col_block):
    extent = cleaned.shape[-1]
    grid_pos = jnp.arange(extent).astype(jnp.float32)
    coord_y = (row_block.astype(jnp.float32) * extent + grid_pos + 0.5) / extent - 1.0
    coord_x = (col_block.astype(jnp.float32) * extent + grid_pos + 0.5) / extent - 1.0
    poly_y = legendre(coord_y)
    poly_x = legendre(coord_x)
    outer_y = (poly_y[:, None, :] * poly_y[None, :, :]).reshape(16, extent).astype(jnp.bfloat16)
    outer_x = (poly_x[:, None, :] * poly_x[None, :, :]).reshape(16, extent).astype(jnp.bfloat16)
    values = cleaned.astype(jnp.float32)
    square = (values * values).astype(jnp.bfloat16)
    row_moment = jnp.dot(outer_y, square, preferred_element_type=jnp.float32)
    return jnp.dot(row_moment, outer_x.astype(jnp.float32).T, precision=precise)


def convolve(image, tap_row, along_columns):
    radius = (tap_row.shape[0] - 1) // 2
    data = image.astype(jnp.float32)[None, None]
    if along_columns:
        kernel = tap_row.astype(jnp.float32)[None, None, None, :]
        padding = ((0, 0), (radius, radius))
    else:
        kernel = tap_row.astype(jnp.float32)[None, None, :, None]
        padding = ((radius, radius), (0, 0))
    result = lax.conv_general_dilated(data, kernel, (1, 1), padding, precision=precise)
    return result[0, 0]


def reference(pixels, row_mask, col_mask, route, tile, wcs_offset, subpixel, plate_scale, stretch_weight, psf_taps):
    ccd_count, visit_count, pieces = route.shape
    extent = pixels.shape[-1]
    patch_side = 2 * extent
    strip_width = PATCHES * patch_side
    kernels = (psf_taps / jnp.sum(psf_taps, axis=2, keepdims=True)).astype(jnp.bfloat16)
    stretch_count = ccd_count * pieces

    def one_visit(carry, visit_now):
        flux_total, weight_total, moments = carry

        def one_stretch(counter, inner):
            layer_sum, weight_acc, moment_acc = inner
            ccd_now = counter // pieces
            piece = counter % pieces
            rows_ok = row_mask[ccd_now, visit_now, piece]
            cols_ok = col_mask[ccd_now, visit_now, piece]
            cleaned = pixels[ccd_now, visit_now, piece] * (rows_ok[:, None] * cols_ok[None, :]).astype(jnp.bfloat16)
            gain_value = stretch_weight[ccd_now, visit_now, piece].astype(jnp.float32)
            warped, row_cover, col_cover = warp_stretch(
                cleaned, plate_scale[ccd_now, visit_now, piece].astype(jnp.float32),
                wcs_offset[ccd_now, visit_now, piece], subpixel[ccd_now, visit_now, piece].astype(jnp.float32),
                gain_value, rows_ok, cols_ok)
            tile_now = tile[ccd_now, visit_now, piece]
            top_row = ((tile_now // 2) * extent).astype(jnp.int32)
            left_col = (route[ccd_now, visit_now, piece] * patch_side + (tile_now % 2) * extent).astype(jnp.int32)
            before = lax.dynamic_slice(layer_sum, (top_row, left_col), (extent, extent))
            layer_sum = lax.dynamic_update_slice(layer_sum, before + warped.astype(jnp.float32), (top_row, left_col))
            cover = row_cover.astype(jnp.float32)[:, None] * col_cover.astype(jnp.float32)[None, :]
            before_weight = lax.dynamic_slice(weight_acc, (top_row, left_col), (extent, extent))
            weight_acc = lax.dynamic_update_slice(weight_acc, before_weight + cover, (top_row, left_col))
            moment_acc = moment_acc.at[ccd_now].add(gain_value * stretch_moments(cleaned, piece // 2, piece % 2))
            return layer_sum, weight_acc, moment_acc

        layer_start = jnp.zeros((patch_side, strip_width), jnp.float32)
        layer_sum, weight_total, moments = lax.fori_loop(0, stretch_count, one_stretch, (layer_start, weight_total, moments))
        layer_image = layer_sum.astype(jnp.bfloat16)
        smooth_x = convolve(layer_image, kernels[visit_now, 0], True).astype(jnp.bfloat16)
        smooth_y = convolve(smooth_x, kernels[visit_now, 1], False)
        return (flux_total + smooth_y, weight_total, moments), None

    start_state = (jnp.zeros((patch_side, strip_width), jnp.float32),
                   jnp.zeros((patch_side, strip_width), jnp.float32),
                   jnp.zeros((ccd_count, 16, 16), jnp.float32))
    final_state, _ = lax.scan(one_visit, start_state, jnp.arange(visit_count))
    coadd_flux, coadd_weight, moments = final_state
    row_pick, col_pick = pick_tables()
    hessian = moments[:, row_pick, col_pick] / (visit_count * pieces * extent * extent)
    return coadd_flux, coadd_weight, hessian
```

```python
import jax
import jax.numpy as jnp
import numpy as np
from jax import lax
from jax.experimental import pallas as pl
from jax.experimental.pallas import tpu as pltpu
from jax.sharding import PartitionSpec as P

PAIRS = ((0, 0), (1, 0), (0, 1), (2, 0), (1, 1), (0, 2), (3, 0), (2, 1), (1, 2), (0, 3))
MESH = pl.DeviceIdType.MESH
precise = lax.Precision.HIGHEST
f32 = jnp.float32
bf16 = jnp.bfloat16
S = 512
TAPS = 41
NP = 16
NV = 8
NS = 8
ROWS = S // NP
HOT = NP - 1


def lanczos(offset):
    inside = jnp.abs(offset) < 3.0
    return jnp.where(inside, jnp.sinc(offset) * jnp.sinc(offset / 3.0), jnp.zeros_like(offset))


def legendre(coord):
    square = coord * coord
    return jnp.stack(
        [jnp.ones_like(coord), coord, 1.5 * square - 0.5, (2.5 * square - 1.5) * coord], axis=-2
    )


def outer_tables():
    grid_pos = jnp.arange(S).astype(f32)
    block = jnp.arange(2).astype(f32)
    coord = (block[:, None] * S + grid_pos[None, :] + 0.5) / S - 1.0
    poly = legendre(coord)
    return (poly[:, :, None, :] * poly[:, None, :, :]).reshape(2, 16, S).astype(bf16)


def dot(a, b, precision=None):
    return jnp.dot(a, b, preferred_element_type=f32, precision=precision)


def dot_nt(a, b, precision=None):
    return lax.dot_general(
        a, b, (((1,), (1,)), ((), ())), preferred_element_type=f32, precision=precision
    )


def dot_tn(a, b):
    return lax.dot_general(a, b, (((0,), (0,)), ((), ())), preferred_element_type=f32)


def band(position, base, weight_of):
    offset = position - base
    value = jnp.zeros(offset.shape, f32)
    for k in range(6):
        value = jnp.where(offset == float(k), weight_of(k), value)
    return value


def tap_matrix(kern, line, shape, shift):
    at = (
        lax.broadcasted_iota(jnp.int32, shape, 0)
        - lax.broadcasted_iota(jnp.int32, shape, 1)
    )
    at = shift(at)

    def one(m, value):
        return jnp.where(at == m, kern[line, m], value)

    return lax.fori_loop(0, TAPS, one, jnp.zeros(shape, f32))


def warp_kernel(
    kern, trow, gain, pix, wts, oy, ox, pp, extra,
    recv, rfr, rsmall, hess, vmat,
    sbuf, fbuf, wpad, ybuf, half, umat, cov, rmom, small, msend, mrecv,
    send_sem, recv_sem, fsend, frecv, ssend, srecv, msend_sem, mrecv_sem,
):
    me_v = lax.axis_index("visit")
    me = lax.axis_index("patch")
    wpad[0:192, :] = jnp.zeros((192, S), bf16)
    wpad[704:896, :] = jnp.zeros((192, S), bf16)
    rmom[...] = jnp.zeros_like(rmom)
    for v in range(2):
        umat[v] = tap_matrix(kern, 2 * v + 1, (128, 256), lambda at: -at - 44).astype(bf16)

    def stretch(s, carry):
        v = s // 4
        piece = s % 4
        is_low = trow[s] == 0
        wt = wts[s]
        columns = jnp.transpose(wt[0:8])
        row_mask = wt[7:8]
        col_mask = wt[15:16]
        ones = jnp.ones((8, 384), bf16)
        for a in range(2):
            at = lax.broadcasted_iota(jnp.int32, (256, 384), 1).astype(f32) + float(128 * a)
            cols = columns[256 * a : 256 * a + 256]
            weights = band(at, cols[:, 6:7], lambda k: cols[:, k : k + 1])
            rows_map = (weights * row_mask[:, 128 * a : 128 * a + 384]).astype(bf16)
            part = dot(rows_map, pix[s, 128 * a : 128 * a + 384, :])
            half[256 * a : 256 * a + 256, :] = (part * col_mask).astype(bf16)
            cover = dot_nt(ones, rows_map)
            cov[pl.ds(s, 1), 256 * a : 256 * a + 256] = cover[0:1]
        for b in range(2):
            at = lax.broadcasted_iota(jnp.int32, (384, 256), 0).astype(f32) + float(128 * b)
            lanes = wt[:, 256 * b : 256 * b + 256]
            cols_map = band(at, lanes[14:15], lambda k: lanes[8 + k : 9 + k]).astype(bf16)
            part = dot(half[:, 128 * b : 128 * b + 384], cols_map)
            wpad[192:704, 256 * b : 256 * b + 256] = part.astype(bf16)
            mask = jnp.broadcast_to(col_mask[:, 128 * b : 128 * b + 384], (8, 384)).astype(bf16)
            cover = dot(mask, cols_map)
            cov[pl.ds(s, 1), S + 256 * b : S + 256 * b + 256] = cover[0:1]
        for a in range(4):
            ybuf[128 * a : 128 * a + 128, :] = dot(
                umat[v], wpad[128 + 128 * a : 384 + 128 * a, :]
            )
        above = dot(umat[v, 96:128, :], wpad[0:256, :])
        below = dot(umat[v, 0:32, :], wpad[640:896, :])
        fbuf[s] = jnp.where(is_low, below, above).astype(bf16)
        for q in range(NP):
            low = ybuf[ROWS * q : ROWS * (q + 1), :]
            high = ybuf[ROWS * (NP - 1 - q) : ROWS * (NP - q), :]
            sbuf[s, ROWS * q : ROWS * (q + 1), :] = jnp.where(is_low, low, high).astype(bf16)

        def send(j, carry):
            k = lax.rem(me + j, NP)
            pltpu.make_async_remote_copy(
                src_ref=sbuf.at[s, pl.ds(pl.multiple_of(k * ROWS, ROWS), ROWS)],
                dst_ref=recv.at[me, s],
                send_sem=send_sem.at[s],
                recv_sem=recv_sem.at[s],
                device_id={"patch": k},
                device_id_type=MESH,
            ).start()
            return carry

        lax.fori_loop(1, NP, send, 0)
        pltpu.make_async_copy(
            sbuf.at[s, pl.ds(pl.multiple_of(me * ROWS, ROWS), ROWS)], recv.at[me, s], recv_sem.at[s]
        ).start()

        @pl.when(me != HOT)
        def _():
            pltpu.make_async_remote_copy(
                src_ref=fbuf.at[s],
                dst_ref=rfr.at[me, s],
                send_sem=fsend.at[s],
                recv_sem=frecv.at[s],
                device_id={"patch": HOT},
                device_id_type=MESH,
            ).start()

        @pl.when(me == HOT)
        def _():
            pltpu.make_async_copy(fbuf.at[s], rfr.at[me, s], frecv.at[s]).start()

        values = pix[s].astype(f32)
        square = (values * values).astype(bf16)
        lhs = oy[piece // 2] * row_mask.astype(bf16)
        rmom[piece % 2] += dot(lhs, square) * (col_mask * gain[s])
        return carry

    lax.fori_loop(0, NS, stretch, 0)

    covers = cov[...].astype(bf16)
    slots = dot(pp[0], covers[:, 0:256])
    for b in range(1, 4):
        slots += dot(pp[b], covers[:, 256 * b : 256 * b + 256])
    small[:, 0:256] = slots
    small[:, 256:384] = extra[...]
    msend[...] = dot_nt(rmom[0], ox[0], precise) + dot_nt(rmom[1], ox[1], precise)

    def send_small(j, carry):
        k = lax.rem(me + j, NP)
        pltpu.make_async_remote_copy(
            src_ref=small.at[pl.ds(pl.multiple_of(k * 8, 8), 8)],
            dst_ref=rsmall.at[me],
            send_sem=ssend,
            recv_sem=srecv,
            device_id={"patch": k},
            device_id_type=MESH,
        ).start()
        return carry

    lax.fori_loop(1, NP, send_small, 0)
    pltpu.make_async_copy(
        small.at[pl.ds(pl.multiple_of(me * 8, 8), 8)], rsmall.at[me], srecv
    ).start()

    def send_moment(j, carry):
        pltpu.make_async_remote_copy(
            src_ref=msend,
            dst_ref=mrecv.at[me_v],
            send_sem=msend_sem,
            recv_sem=mrecv_sem,
            device_id={"visit": lax.rem(me_v + j, NV)},
            device_id_type=MESH,
        ).start()
        return carry

    lax.fori_loop(1, NV, send_moment, 0)
    pltpu.make_async_copy(msend, mrecv.at[me_v], mrecv_sem).start()

    for v in range(2):
        for c in range(4):
            vmat[v, 128 * c : 128 * c + 128, :] = tap_matrix(
                kern, 2 * v, (128, 256), lambda at: at + (128 * c - 108)
            ).astype(bf16)

    pltpu.make_async_copy(mrecv, mrecv, mrecv_sem).wait()
    total = mrecv[0]
    for v in range(1, NV):
        total += mrecv[v]
    hess[...] = total
    pltpu.make_async_copy(mrecv.at[1:NV], mrecv.at[1:NV], msend_sem).wait()
    pltpu.make_async_copy(rsmall, rsmall, srecv).wait()
    pltpu.make_async_copy(rsmall.at[1:NP], rsmall.at[1:NP], ssend).wait()

    def finish(s, carry):
        everyone = recv.at[:, s]
        others = recv.at[1:NP, s]
        pltpu.make_async_copy(everyone, everyone, recv_sem.at[s]).wait()
        pltpu.make_async_copy(others, others, send_sem.at[s]).wait()

        @pl.when(me != HOT)
        def _():
            pltpu.make_async_copy(fbuf.at[s], fbuf.at[s], fsend.at[s]).wait()

        @pl.when(me == HOT)
        def _():
            pltpu.make_async_copy(rfr.at[:, s], rfr.at[:, s], frecv.at[s]).wait()

        return carry

    lax.fori_loop(0, NS, finish, 0)


def layer_kernel(codes, recv, rfr, vmat, out, acc, fvm, sem):
    me = lax.axis_index("patch")
    zero = jnp.zeros((ROWS, 256), f32)

    def clear(b, carry):
        for v in range(2):
            for t in range(2):
                acc[v, t, b] = zero
        return carry

    lax.fori_loop(0, 66, clear, 0)

    def place(at, s, value, flip):
        code = codes[at]
        tile = code % 4
        g = 2 * (code // 4) + tile % 2
        t = tile // 2
        if flip:
            t = 1 - t
        data = value.astype(f32)
        acc[s // 4, t, 2 * g + 1] += data[:, 0:256]
        acc[s // 4, t, 2 * g + 2] += data[:, 256:512]

    def add(at, carry):
        s = at % NS
        place(at, s, recv[at // NS, s], False)
        return carry

    lax.fori_loop(0, NP * NS, add, 0)

    @pl.when(me == HOT)
    def _():
        copy = pltpu.make_async_copy(rfr, fvm, sem)
        copy.start()
        copy.wait()

        def add_fringe(at, carry):
            s = at % NS
            place(at, s, fvm[at // NS, s], True)
            return carry

        lax.fori_loop(0, NP * NS, add_fringe, 0)

    for t in range(2):
        for c in range(4):
            total = None
            for v in range(2):
                block = acc[v, t, 16 * c : 16 * c + 18].reshape(18 * ROWS, 256).astype(bf16)
                left = block[0 : 16 * ROWS, 128:256]
                middle = block[ROWS : 17 * ROWS]
                right = block[2 * ROWS : 18 * ROWS, 0:128]
                part = dot(middle, vmat[v, 128:384])
                part += dot(left, vmat[v, 0:128])
                part += dot(right, vmat[v, 384:512])
                total = part if total is None else total + part
            out[t, 16 * c : 16 * c + 16] = total.astype(bf16).reshape(16, ROWS, 256)


def owner_kernel(slab, wmsg, flux, weight, frecv, wrecv, send_sem, recv_sem, wsend_sem, wrecv_sem):
    me_v = lax.axis_index("visit")
    me = lax.axis_index("patch")
    for t in range(2):
        block = me if t == 0 else NP - 1 - me
        r = 4 * t + block // 4
        slot = lax.rem(block, 4)

        def send(j, carry):
            p = lax.rem(me + j, NP)
            src = slab.at[t, pl.ds(4 * p, 4)]
            dst = frecv.at[me_v, slot]
            mine = (r == me_v) & (p == me)

            @pl.when(jnp.logical_not(mine))
            def _():
                pltpu.make_async_remote_copy(
                    src_ref=src,
                    dst_ref=dst,
                    send_sem=send_sem,
                    recv_sem=recv_sem,
                    device_id={"visit": r, "patch": p},
                    device_id_type=MESH,
                ).start()

            @pl.when(mine)
            def _():
                pltpu.make_async_copy(src, dst, recv_sem).start()

            return carry

        lax.fori_loop(0, NP, send, 0)

    def send_weight(j, carry):
        r = lax.rem(me_v + j, NV)
        pltpu.make_async_remote_copy(
            src_ref=wmsg.at[r],
            dst_ref=wrecv.at[me_v],
            send_sem=wsend_sem,
            recv_sem=wrecv_sem,
            device_id={"visit": r},
            device_id_type=MESH,
        ).start()
        return carry

    lax.fori_loop(1, NV, send_weight, 0)
    pltpu.make_async_copy(wmsg.at[me_v], wrecv.at[me_v], wrecv_sem).start()
    pltpu.make_async_copy(wrecv, wrecv, wrecv_sem).wait()
    cols = wrecv[:, :, 0:512].reshape(NV * 2 * NP, 512)
    left = wrecv[:, :, 512:640].reshape(NV * 2 * NP, 128)
    right = wrecv[:, :, 640:768].reshape(NV * 2 * NP, 128)
    weight[:, 0:512] = dot_tn(left, cols)
    weight[:, 512:1024] = dot_tn(right, cols)
    pltpu.make_async_copy(frecv, frecv, recv_sem).wait()
    for slot in range(4):
        for q in range(4):
            total = frecv[0, slot, q].astype(f32)
            for v in range(1, NV):
                total += frecv[v, slot, q].astype(f32)
            flux[32 * slot : 32 * slot + 32, 256 * q : 256 * q + 256] = total
    pltpu.make_async_copy(wrecv.at[1:NV], wrecv.at[1:NV], wsend_sem).wait()
    is_mine = (me_v == me // 4) | (me_v == 4 + (NP - 1 - me) // 4)

    @pl.when(is_mine)
    def _():
        pltpu.make_async_copy(slab.at[0, 0:60], slab.at[0, 0:60], send_sem).wait()
        pltpu.make_async_copy(slab.at[1], slab.at[1], send_sem).wait()

    @pl.when(jnp.logical_not(is_mine))
    def _():
        pltpu.make_async_copy(slab, slab, send_sem).wait()


def body(
    pixels, row_mask, col_mask, route, tile, wcs_offset, subpixel, plate_scale, stretch_weight, psf_taps
):
    pix = pixels.reshape(NS, S, S)
    route = route.reshape(NS)
    tile = tile.reshape(NS)
    gain = stretch_weight.reshape(NS).astype(f32)
    scale = plate_scale.reshape(NS, 1, 1).astype(f32)
    shift = wcs_offset.reshape(NS, 2, 1).astype(f32) + subpixel.reshape(NS, 2, 1).astype(f32)
    grid_pos = jnp.arange(S).astype(f32)
    middle = S / 2.0
    source = scale * (grid_pos - middle) + (middle + shift)
    lowest = jnp.floor(source) - 2.0
    taps = jnp.arange(6).astype(f32)[None, None, :, None]
    factor = jnp.stack([jnp.ones_like(gain), gain], axis=1)[:, :, None, None]
    spots = lowest[:, :, None, :] + taps
    weights = (factor * lanczos(spots - source[:, :, None, :])).astype(bf16).astype(f32)
    masks = jnp.stack([row_mask.reshape(NS, S), col_mask.reshape(NS, S)], axis=1).astype(f32)
    wts = jnp.concatenate([weights, lowest[:, :, None], masks[:, :, None]], axis=2)
    wts = wts.reshape(NS, 16, S)
    kern = (psf_taps / jnp.sum(psf_taps, axis=2, keepdims=True)).astype(bf16).astype(f32)
    kern = kern.reshape(4, TAPS)

    order = jnp.arange(NS)
    rank = jnp.sum(
        (route[:, None] == route[None, :]) & (order[None, :] < order[:, None]), axis=1
    )
    line = jnp.arange(8 * NP)
    here = (route[None, :] == line[:, None] // 8) & (rank[None, :] == line[:, None] % 8 // 4)
    pp = (
        here[None] & ((line % 4)[None, :, None] == jnp.arange(4)[:, None, None])
    ).astype(bf16)
    slot_tile = jnp.sum(here * tile[None, :], axis=1).astype(f32)
    code = (route * 4 + tile).astype(f32)
    code_line = jnp.broadcast_to(code[None, :], (NP, 8)).reshape(8 * NP)
    extra = jnp.where(jnp.arange(128)[None, :] == 0, code_line[:, None], slot_tile[:, None])

    outer = outer_tables()
    outer_x = jnp.pad(outer.astype(f32), ((0, 0), (0, 112), (0, 0)))
    vm = pl.BlockSpec(memory_space=pltpu.VMEM)
    sm = pl.BlockSpec(memory_space=pltpu.SMEM)
    hbm = pl.BlockSpec(memory_space=pl.ANY)
    dma = pltpu.SemaphoreType.DMA
    recv, rfr, rsmall, moments, vmat = pl.pallas_call(
        warp_kernel,
        out_shape=(
            jax.ShapeDtypeStruct((NP, NS, ROWS, S), bf16),
            jax.ShapeDtypeStruct((NP, NS, ROWS, S), bf16),
            jax.ShapeDtypeStruct((NP, 8, 384), f32),
            jax.ShapeDtypeStruct((16, 128), f32),
            jax.ShapeDtypeStruct((2, 512, 256), bf16),
        ),
        in_specs=[sm, sm, sm, vm, vm, vm, vm, vm, vm],
        out_specs=(hbm, hbm, hbm, vm, vm),
        scratch_shapes=[
            pltpu.VMEM((NS, S, S), bf16),
            pltpu.VMEM((NS, ROWS, S), bf16),
            pltpu.VMEM((896, S), bf16),
            pltpu.VMEM((S, S), f32),
            pltpu.VMEM((S, S), bf16),
            pltpu.VMEM((2, 128, 256), bf16),
            pltpu.VMEM((8, 2 * S), f32),
            pltpu.VMEM((2, 16, S), f32),
            pltpu.VMEM((128, 384), f32),
            pltpu.VMEM((16, 128), f32),
            pltpu.VMEM((NV, 16, 128), f32),
            dma((NS,)), dma((NS,)), dma((NS,)), dma((NS,)),
            dma, dma, dma, dma,
        ],
        compiler_params=pltpu.CompilerParams(
            has_side_effects=True, vmem_limit_bytes=48 * 1024 * 1024
        ),
        name="warp_send",
    )(kern, tile // 2, gain, pix, wts, outer, outer_x, pp, extra)

    codes = rsmall[:, :, 256].reshape(NP * NS).astype(jnp.int32)
    slab = pl.pallas_call(
        layer_kernel,
        out_shape=jax.ShapeDtypeStruct((2, 64, ROWS, 256), bf16),
        in_specs=[sm, vm, hbm, vm],
        out_specs=vm,
        scratch_shapes=[
            pltpu.VMEM((2, 2, 66, ROWS, 256), f32),
            pltpu.VMEM((NP, NS, ROWS, S), bf16),
            dma,
        ],
        compiler_params=pltpu.CompilerParams(vmem_limit_bytes=48 * 1024 * 1024),
        name="layer_smooth",
    )(codes, recv, rfr, vmat)

    covers = rsmall[:, :, 0:256].reshape(2 * NP, 2 * S)
    tiles = rsmall[:, ::4, 257].reshape(1, 2 * NP, 1, 1).astype(jnp.int32)
    owner = jnp.arange(NV)[:, None, None, None]
    keep = (tiles // 2 == owner // 4) & (tiles % 2 == jnp.arange(2)[None, None, :, None])
    row_part = covers[:, :S].reshape(2 * NP, 4, 128).transpose(1, 0, 2)
    row_part = jnp.concatenate([row_part, row_part], axis=0)
    row_part = jnp.where(keep, row_part[:, :, None, :], 0.0).reshape(NV, 2 * NP, 256)
    col_part = jnp.broadcast_to(covers[None, :, S:], (NV, 2 * NP, S))
    wmsg = jnp.concatenate([col_part, row_part], axis=2).astype(bf16)

    flux, weight = pl.pallas_call(
        owner_kernel,
        out_shape=(
            jax.ShapeDtypeStruct((128, 2 * S), f32),
            jax.ShapeDtypeStruct((128, 2 * S), f32),
        ),
        in_specs=[vm, vm],
        out_specs=(vm, vm),
        scratch_shapes=[
            pltpu.VMEM((NV, 4, 4, ROWS, 256), bf16),
            pltpu.VMEM((NV, 2 * NP, 768), bf16),
            dma, dma, dma, dma,
        ],
        compiler_params=pltpu.CompilerParams(
            has_side_effects=True, vmem_limit_bytes=48 * 1024 * 1024
        ),
        name="owner_sum",
    )(slab, wmsg)

    norm_factor = 1.0 / (NV * 2 * 4 * S * S)
    first = np.array([pair[0] for pair in PAIRS])
    second = np.array([pair[1] for pair in PAIRS])
    pick_row = np.zeros((100, 16), np.float32)
    pick_col = np.zeros((100, 16), np.float32)
    for q in range(10):
        for r in range(10):
            pick_row[10 * q + r, 4 * first[q] + first[r]] = 1
            pick_col[10 * q + r, 4 * second[q] + second[r]] = 1
    picked = jnp.dot(pick_row, moments[:, :16], precision=precise)
    hessian = jnp.sum(picked * pick_col, axis=1).reshape(1, 10, 10) * norm_factor
    return flux, weight, hessian


def solution(mesh):
    in_specs = (
        P("patch", "visit", None, None, None),
        P("patch", "visit", None, None),
        P("patch", "visit", None, None),
        P("patch", "visit", None),
        P("patch", "visit", None),
        P("patch", "visit", None, None),
        P("patch", "visit", None, None),
        P("patch", "visit", None),
        P("patch", "visit", None),
        P("visit", None, None),
    )
    out_specs = (P("visit", "patch"), P("visit", "patch"), P("patch", None, None))
    return jax.shard_map(body, mesh=mesh, in_specs=in_specs, out_specs=out_specs, check_vma=False)
```

```python
import jax
import jax.numpy as jnp
import numpy as np
from jax import lax
from jax.experimental import pallas as pl
from jax.experimental.pallas import tpu as pltpu
from jax.sharding import PartitionSpec as P

PAIRS = ((0, 0), (1, 0), (0, 1), (2, 0), (1, 1), (0, 2), (3, 0), (2, 1), (1, 2), (0, 3))
MESH = pl.DeviceIdType.MESH
precise = lax.Precision.HIGHEST
f32 = jnp.float32
bf16 = jnp.bfloat16
S = 512
TAPS = 41
NP = 16
NV = 8
NS = 8
ROWS = S // NP
SPILL = 10


def lanczos(offset):
    inside = jnp.abs(offset) < 3.0
    return jnp.where(inside, jnp.sinc(offset) * jnp.sinc(offset / 3.0), jnp.zeros_like(offset))


def legendre(coord):
    square = coord * coord
    return jnp.stack(
        [jnp.ones_like(coord), coord, 1.5 * square - 0.5, (2.5 * square - 1.5) * coord], axis=-2
    )


def outer_tables():
    grid_pos = jnp.arange(S).astype(f32)
    block = jnp.arange(2).astype(f32)
    coord = (block[:, None] * S + grid_pos[None, :] + 0.5) / S - 1.0
    poly = legendre(coord)
    return (poly[:, :, None, :] * poly[:, None, :, :]).reshape(2, 16, S).astype(bf16)


def dot(a, b, precision=None):
    return jnp.dot(a, b, preferred_element_type=f32, precision=precision)


def dot_nt(a, b, precision=None):
    return lax.dot_general(
        a, b, (((1,), (1,)), ((), ())), preferred_element_type=f32, precision=precision
    )


def dot_tn(a, b):
    return lax.dot_general(a, b, (((0,), (0,)), ((), ())), preferred_element_type=f32)


def band(position, base, weight_of):
    offset = position - base
    value = jnp.zeros(offset.shape, f32)
    for k in range(6):
        value = jnp.where(offset == float(k), weight_of(k), value)
    return value


def spill_row(row):
    return 2 * (row // 16) + row % 2


def tap_matrix(kern, line, shape, tap_of):
    at = tap_of(
        lax.broadcasted_iota(jnp.int32, shape, 0), lax.broadcasted_iota(jnp.int32, shape, 1)
    )

    def one(m, value):
        return jnp.where(at == m, kern[line, m], value)

    return lax.fori_loop(0, TAPS, one, jnp.zeros(shape, f32))


def warp_kernel(
    kern, trow, gain, pix, wts, ylines, oy, ox, pp, extra,
    recv, rfr, rsmall, hess, vmat,
    sbuf, fbuf, wpad, ybuf, half, edges, umat, cov, rmom, small, msend, mrecv,
    send_sem, recv_sem, fsend, frecv, ssend, srecv, msend_sem, mrecv_sem,
):
    me_v = lax.axis_index("visit")
    me = lax.axis_index("patch")
    wpad[0:192, :] = jnp.zeros((192, S), bf16)
    wpad[704:896, :] = jnp.zeros((192, S), bf16)
    rmom[...] = jnp.zeros_like(rmom)
    for v in range(2):
        line = jnp.broadcast_to(ylines[v : v + 1], (128, 256))
        umat[v] = pltpu.roll(line, 0, 1, stride=1, stride_axis=0).astype(bf16)

    def stretch(s):
        v = s // 4
        is_low = trow[s] == 0
        wt = wts[s]
        columns = jnp.transpose(wt[0:8])
        row_mask = wt[7:8]
        col_mask = wt[15:16]
        ones = jnp.ones((8, 384), bf16)
        for a in range(2):
            at = lax.broadcasted_iota(jnp.int32, (256, 384), 1).astype(f32) + float(128 * a)
            cols = columns[256 * a : 256 * a + 256]
            weights = band(at, cols[:, 6:7], lambda k: cols[:, k : k + 1])
            rows_map = (weights * row_mask[:, 128 * a : 128 * a + 384]).astype(bf16)
            part = dot(rows_map, pix[s, 128 * a : 128 * a + 384, :])
            half[256 * a : 256 * a + 256, :] = (part * col_mask).astype(bf16)
            cover = dot_nt(ones, rows_map)
            cov[pl.ds(s, 1), 256 * a : 256 * a + 256] = cover[0:1]
        for b in range(2):
            at = lax.broadcasted_iota(jnp.int32, (384, 256), 0).astype(f32) + float(128 * b)
            lanes = wt[:, 256 * b : 256 * b + 256]
            cols_map = band(at, lanes[14:15], lambda k: lanes[8 + k : 9 + k]).astype(bf16)
            part = dot(half[:, 128 * b : 128 * b + 384], cols_map)
            wpad[192:704, 256 * b : 256 * b + 256] = part.astype(bf16)
            mask = jnp.broadcast_to(col_mask[:, 128 * b : 128 * b + 384], (8, 384)).astype(bf16)
            cover = dot(mask, cols_map)
            cov[pl.ds(s, 1), S + 256 * b : S + 256 * b + 256] = cover[0:1]
        for a in range(4):
            ybuf[128 * a : 128 * a + 128, :] = dot(
                umat[v], wpad[128 + 128 * a : 384 + 128 * a, :]
            ).astype(bf16)
        for q in range(NP):
            low = ybuf[ROWS * q : ROWS * (q + 1), :]
            high = ybuf[ROWS * (NP - 1 - q) : ROWS * (NP - q), :]
            sbuf[s, ROWS * q : ROWS * (q + 1), :] = jnp.where(is_low, low, high)
        edges[s, 0:64] = wpad[192:256, :]
        edges[s, 64:128] = wpad[640:704, :]

    turn = 7 * me + 3 * me_v

    def step(s, carry):
        stretch(s)

        def send(j, carry):
            k = lax.rem(me + 1 + lax.rem(turn + j, NP - 1), NP)
            pltpu.make_async_remote_copy(
                src_ref=sbuf.at[s, pl.ds(pl.multiple_of(k * ROWS, ROWS), ROWS)],
                dst_ref=recv.at[me, s],
                send_sem=send_sem.at[s],
                recv_sem=recv_sem.at[s],
                device_id={"patch": k},
                device_id_type=MESH,
            ).start()
            return carry

        lax.fori_loop(0, NP - 1, send, 0)
        pltpu.make_async_copy(
            sbuf.at[s, pl.ds(pl.multiple_of(me * ROWS, ROWS), ROWS)], recv.at[me, s], recv_sem.at[s]
        ).start()
        return carry

    lax.fori_loop(0, NS, step, 0)

    row = lax.broadcasted_iota(jnp.int32, (16 * SPILL, 128), 0)
    lane = lax.broadcasted_iota(jnp.int32, (16 * SPILL, 128), 1)
    spilled = jnp.zeros((16 * SPILL, S), f32)
    for v in range(2):
        taps = tap_matrix(
            kern,
            2 * v + 1,
            (16 * SPILL, 128),
            lambda row, lane: jnp.where(
                lane >= 64, lane - spill_row(row) - 108, lane + spill_row(row) + 21
            ),
        )
        for s in range(4 * v, 4 * v + 4):
            keep = (row % 16 // 2 == s) & (lane // 64 == 1 - trow[s])
            spilled += dot(jnp.where(keep, taps, 0.0).astype(bf16), edges[s])
    fbuf[...] = spilled.astype(bf16)

    def send_spill(k, carry):
        src = fbuf.at[pl.ds(pl.multiple_of(16 * k, 16), 16)]

        @pl.when(me != k)
        def _():
            pltpu.make_async_remote_copy(
                src_ref=src,
                dst_ref=rfr.at[me],
                send_sem=fsend,
                recv_sem=frecv,
                device_id={"patch": k},
                device_id_type=MESH,
            ).start()

        @pl.when(me == k)
        def _():
            pltpu.make_async_copy(src, rfr.at[me], frecv).start()

        return carry

    lax.fori_loop(0, SPILL, send_spill, 0)

    def moments(s, carry):
        piece = s % 4
        values = pix[s].astype(f32)
        square = (values * values).astype(bf16)
        lhs = oy[piece // 2] * wts[s, 7:8].astype(bf16)
        rmom[piece % 2] += dot(lhs, square) * (wts[s, 15:16] * gain[s])
        return carry

    lax.fori_loop(0, NS, moments, 0)
    covers = cov[...].astype(bf16)
    slots = dot(pp[0], covers[:, 0:256])
    for b in range(1, 4):
        slots += dot(pp[b], covers[:, 256 * b : 256 * b + 256])
    small[:, 0:256] = slots
    small[:, 256:384] = extra[...]
    msend[...] = dot_nt(rmom[0], ox[0], precise) + dot_nt(rmom[1], ox[1], precise)

    def send_small(j, carry):
        k = lax.rem(me + j, NP)
        pltpu.make_async_remote_copy(
            src_ref=small.at[pl.ds(pl.multiple_of(k * 8, 8), 8)],
            dst_ref=rsmall.at[me],
            send_sem=ssend,
            recv_sem=srecv,
            device_id={"patch": k},
            device_id_type=MESH,
        ).start()
        return carry

    lax.fori_loop(1, NP, send_small, 0)
    pltpu.make_async_copy(
        small.at[pl.ds(pl.multiple_of(me * 8, 8), 8)], rsmall.at[me], srecv
    ).start()

    def send_moment(j, carry):
        pltpu.make_async_remote_copy(
            src_ref=msend,
            dst_ref=mrecv.at[me_v],
            send_sem=msend_sem,
            recv_sem=mrecv_sem,
            device_id={"visit": lax.rem(me_v + j, NV)},
            device_id_type=MESH,
        ).start()
        return carry

    lax.fori_loop(1, NV, send_moment, 0)
    pltpu.make_async_copy(msend, mrecv.at[me_v], mrecv_sem).start()

    for v in range(2):
        for c in range(4):
            vmat[v, 128 * c : 128 * c + 128, :] = tap_matrix(
                kern, 2 * v, (128, 256), lambda row, lane: row - lane + (128 * c - 108)
            ).astype(bf16)

    pltpu.make_async_copy(mrecv, mrecv, mrecv_sem).wait()
    total = mrecv[0]
    for v in range(1, NV):
        total += mrecv[v]
    hess[...] = total
    pltpu.make_async_copy(mrecv.at[1:NV], mrecv.at[1:NV], msend_sem).wait()
    pltpu.make_async_copy(rsmall, rsmall, srecv).wait()
    pltpu.make_async_copy(rsmall.at[1:NP], rsmall.at[1:NP], ssend).wait()

    def finish(i, carry):
        everyone = recv.at[:, i]
        others = recv.at[1:NP, i]
        pltpu.make_async_copy(everyone, everyone, recv_sem.at[i]).wait()
        pltpu.make_async_copy(others, others, send_sem.at[i]).wait()
        return carry

    lax.fori_loop(0, NS, finish, 0)

    @pl.when(me < SPILL)
    def _():
        others = fbuf.at[0 : 16 * (SPILL - 1)]
        pltpu.make_async_copy(rfr, rfr, frecv).wait()
        pltpu.make_async_copy(others, others, fsend).wait()

    @pl.when(me >= SPILL)
    def _():
        pltpu.make_async_copy(fbuf, fbuf, fsend).wait()


def layer_kernel(codes, recv, rfr, vmat, out, outf, acc, accf, fvm, sem):
    me = lax.axis_index("patch")
    zero = jnp.zeros((ROWS, 256), f32)

    def clear(b, carry):
        for v in range(2):
            for t in range(2):
                acc[v, t, b] = zero
        return carry

    lax.fori_loop(0, 66, clear, 0)

    def add(at, carry):
        s = at % NS
        code = codes[at]
        tile = code % 4
        g = 2 * (code // 4) + tile % 2
        t = tile // 2
        data = recv[at // NS, s].astype(f32)
        acc[s // 4, t, 2 * g + 1] += data[:, 0:256]
        acc[s // 4, t, 2 * g + 2] += data[:, 256:512]
        return carry

    lax.fori_loop(0, NP * NS, add, 0)

    def smooth(blocks_of, count):
        total = None
        rows = blocks_of(0).shape[0] // (count + 2)
        for v in range(2):
            block = blocks_of(v)
            part = dot(block[rows : (count + 1) * rows], vmat[v, 128:384])
            part += dot(block[0 : count * rows, 128:256], vmat[v, 0:128])
            part += dot(block[2 * rows : (count + 2) * rows, 0:128], vmat[v, 384:512])
            total = part if total is None else total + part
        return total.astype(bf16)

    for t in range(2):
        for c in range(4):
            total = smooth(
                lambda v: acc[v, t, 16 * c : 16 * c + 18].reshape(18 * ROWS, 256).astype(bf16), 16
            )
            out[t, 16 * c : 16 * c + 16] = total.reshape(16, ROWS, 256)

    @pl.when(me < SPILL)
    def _():
        copy = pltpu.make_async_copy(rfr, fvm, sem)
        copy.start()
        accf[...] = jnp.zeros_like(accf)
        copy.wait()
        target = lax.broadcasted_iota(jnp.int32, (8, S), 0) // 2

        def add_spill(c, carry):
            rows = fvm[c].astype(f32)
            for s in range(NS):
                code = codes[c * NS + s]
                tile = code % 4
                g = 2 * (code // 4) + tile % 2
                two = rows[2 * s : 2 * s + 2]
                data = jnp.where(
                    target == 1 - tile // 2, jnp.concatenate([two, two, two, two], axis=0), 0.0
                )
                accf[s // 4, 2 * g + 1] += data[:, 0:256]
                accf[s // 4, 2 * g + 2] += data[:, 256:512]
            return carry

        lax.fori_loop(0, NP, add_spill, 0)
        outf[...] = smooth(lambda v: accf[v].reshape(66 * 8, 256).astype(bf16), 64)


def owner_kernel(
    slab, spill, wmsg, flux, weight,
    part, summed, frecv, wrecv, spart, ssum, srecv,
    part_send, part_recv, sum_send, sum_recv, wsend_sem, wrecv_sem,
    spart_send, spart_recv, ssum_send, ssum_recv,
):
    me_v = lax.axis_index("visit")
    me = lax.axis_index("patch")

    turn = 3 * me_v + 2 * me

    def group(v):
        return lax.rem(v + me // 2, NV)

    mine_group = group(me_v)

    for t in range(2):

        def send_part(j, carry):
            r = lax.rem(me_v + 1 + lax.rem(turn + j, NV - 1), NV)
            pltpu.make_async_remote_copy(
                src_ref=slab.at[t, pl.ds(8 * group(r), 8)],
                dst_ref=part.at[t, me_v],
                send_sem=part_send.at[t],
                recv_sem=part_recv.at[t],
                device_id={"visit": r},
                device_id_type=MESH,
            ).start()
            return carry

        lax.fori_loop(0, NV - 1, send_part, 0)
        pltpu.make_async_copy(
            slab.at[t, pl.ds(8 * mine_group, 8)], part.at[t, me_v], part_recv.at[t]
        ).start()

    @pl.when(me < SPILL)
    def _():
        def send_spill(j, carry):
            r = lax.rem(me_v + j, NV)
            pltpu.make_async_remote_copy(
                src_ref=spill.at[pl.ds(pl.multiple_of(64 * group(r), 64), 64)],
                dst_ref=spart.at[me_v],
                send_sem=spart_send,
                recv_sem=spart_recv,
                device_id={"visit": r},
                device_id_type=MESH,
            ).start()
            return carry

        lax.fori_loop(1, NV, send_spill, 0)
        pltpu.make_async_copy(
            spill.at[pl.ds(pl.multiple_of(64 * mine_group, 64), 64)], spart.at[me_v], spart_recv
        ).start()

    def send_weight(j, carry):
        r = lax.rem(me_v + j, NV)
        pltpu.make_async_remote_copy(
            src_ref=wmsg.at[r],
            dst_ref=wrecv.at[me_v],
            send_sem=wsend_sem,
            recv_sem=wrecv_sem,
            device_id={"visit": r},
            device_id_type=MESH,
        ).start()
        return carry

    lax.fori_loop(1, NV, send_weight, 0)
    pltpu.make_async_copy(wmsg.at[me_v], wrecv.at[me_v], wrecv_sem).start()

    for t in range(2):
        block = me if t == 0 else NP - 1 - me
        r = 4 * t + block // 4
        slot = lax.rem(block, 4)
        pltpu.make_async_copy(part.at[t], part.at[t], part_recv.at[t]).wait()

        def add(b, carry):
            total = part[t, 0, b].astype(f32)
            for v in range(1, NV):
                total += part[t, v, b].astype(f32)
            summed[t, b] = total.astype(bf16)
            return carry

        lax.fori_loop(0, 8, add, 0)
        for half in range(2):
            p = 2 * mine_group + half
            mine = (r == me_v) & (p == me)
            src = summed.at[t, 4 * half : 4 * half + 4]

            @pl.when(jnp.logical_not(mine))
            def _():
                pltpu.make_async_remote_copy(
                    src_ref=src,
                    dst_ref=frecv.at[slot],
                    send_sem=sum_send.at[t, half],
                    recv_sem=sum_recv,
                    device_id={"visit": r, "patch": p},
                    device_id_type=MESH,
                ).start()

            @pl.when(mine)
            def _():
                pltpu.make_async_copy(src, frecv.at[slot], sum_recv).start()

    def spill_legs(act):
        for half in range(2):
            for t in range(2):
                act(half, t, (me_v == 3 + t) & (me == 2 * mine_group + half))

    @pl.when(me < SPILL)
    def _():
        pltpu.make_async_copy(spart, spart, spart_recv).wait()
        total = spart[0].astype(f32)
        for v in range(1, NV):
            total += spart[v].astype(f32)
        ssum[...] = total

        def leg(half, t, mine):
            src = ssum.at[32 * half : 32 * half + 32]

            @pl.when(jnp.logical_not(mine))
            def _():
                pltpu.make_async_remote_copy(
                    src_ref=src,
                    dst_ref=srecv.at[me],
                    send_sem=ssum_send.at[t, half],
                    recv_sem=ssum_recv,
                    device_id={"visit": 3 + t, "patch": 2 * mine_group + half},
                    device_id_type=MESH,
                ).start()

            @pl.when(mine)
            def _():
                pltpu.make_async_copy(src, srecv.at[me], ssum_recv).start()

        spill_legs(leg)

    pltpu.make_async_copy(wrecv, wrecv, wrecv_sem).wait()
    cols = wrecv[:, :, 0:512].reshape(NV * 2 * NP, 512)
    left = wrecv[:, :, 512:640].reshape(NV * 2 * NP, 128)
    right = wrecv[:, :, 640:768].reshape(NV * 2 * NP, 128)
    weight[:, 0:512] = dot_tn(left, cols)
    weight[:, 512:1024] = dot_tn(right, cols)
    pltpu.make_async_copy(frecv, frecv, sum_recv).wait()
    for slot in range(4):
        for q in range(4):
            flux[32 * slot : 32 * slot + 32, 256 * q : 256 * q + 256] = frecv[slot, q].astype(f32)
    for t in range(2):

        @pl.when(me_v == 3 + t)
        def _():
            pltpu.make_async_copy(srecv, srecv, ssum_recv).wait()
            for k in range(SPILL):
                for e in range(2):
                    at = 2 * k + e
                    line = at if t == 1 else 127 - at
                    for q in range(4):
                        flux[line : line + 1, 256 * q : 256 * q + 256] += srecv[
                            k, 8 * q + 2 * t + e : 8 * q + 2 * t + e + 1, :
                        ]

    @pl.when(me < SPILL)
    def _():
        pltpu.make_async_copy(spart.at[1:NV], spart.at[1:NV], spart_send).wait()

        def leg_sent(half, t, mine):
            @pl.when(jnp.logical_not(mine))
            def _():
                src = ssum.at[32 * half : 32 * half + 32]
                pltpu.make_async_copy(src, src, ssum_send.at[t, half]).wait()

        spill_legs(leg_sent)

    pltpu.make_async_copy(wrecv.at[1:NV], wrecv.at[1:NV], wsend_sem).wait()
    for t in range(2):
        block = me if t == 0 else NP - 1 - me
        r = 4 * t + block // 4
        pltpu.make_async_copy(part.at[t, 1:NV], part.at[t, 1:NV], part_send.at[t]).wait()
        for half in range(2):
            mine = (r == me_v) & (2 * mine_group + half == me)

            @pl.when(jnp.logical_not(mine))
            def _():
                src = summed.at[t, 4 * half : 4 * half + 4]
                pltpu.make_async_copy(src, src, sum_send.at[t, half]).wait()


def body(
    pixels, row_mask, col_mask, route, tile, wcs_offset, subpixel, plate_scale, stretch_weight, psf_taps
):
    pix = pixels.reshape(NS, S, S)
    route = route.reshape(NS)
    tile = tile.reshape(NS)
    gain = stretch_weight.reshape(NS).astype(f32)
    scale = plate_scale.reshape(NS, 1, 1).astype(f32)
    shift = wcs_offset.reshape(NS, 2, 1).astype(f32) + subpixel.reshape(NS, 2, 1).astype(f32)
    grid_pos = jnp.arange(S).astype(f32)
    middle = S / 2.0
    source = scale * (grid_pos - middle) + (middle + shift)
    lowest = jnp.floor(source) - 2.0
    taps = jnp.arange(6).astype(f32)[None, None, :, None]
    factor = jnp.stack([jnp.ones_like(gain), gain], axis=1)[:, :, None, None]
    spots = lowest[:, :, None, :] + taps
    weights = (factor * lanczos(spots - source[:, :, None, :])).astype(bf16).astype(f32)
    masks = jnp.stack([row_mask.reshape(NS, S), col_mask.reshape(NS, S)], axis=1).astype(f32)
    wts = jnp.concatenate([weights, lowest[:, :, None], masks[:, :, None]], axis=2)
    wts = wts.reshape(NS, 16, S)
    kern = (psf_taps / jnp.sum(psf_taps, axis=2, keepdims=True)).astype(bf16).astype(f32)
    ylines = jnp.pad(kern[:, 1], ((0, 0), (44, 256 - 44 - TAPS)))
    kern = kern.reshape(4, TAPS)

    order = jnp.arange(NS)
    rank = jnp.sum(
        (route[:, None] == route[None, :]) & (order[None, :] < order[:, None]), axis=1
    )
    line = jnp.arange(8 * NP)
    here = (route[None, :] == line[:, None] // 8) & (rank[None, :] == line[:, None] % 8 // 4)
    pp = (
        here[None] & ((line % 4)[None, :, None] == jnp.arange(4)[:, None, None])
    ).astype(bf16)
    slot_tile = jnp.sum(here * tile[None, :], axis=1).astype(f32)
    code = (route * 4 + tile).astype(f32)
    code_line = jnp.broadcast_to(code[None, :], (NP, 8)).reshape(8 * NP)
    extra = jnp.where(jnp.arange(128)[None, :] == 0, code_line[:, None], slot_tile[:, None])

    outer = outer_tables()
    outer_x = jnp.pad(outer.astype(f32), ((0, 0), (0, 112), (0, 0)))
    vm = pl.BlockSpec(memory_space=pltpu.VMEM)
    sm = pl.BlockSpec(memory_space=pltpu.SMEM)
    hbm = pl.BlockSpec(memory_space=pl.ANY)
    dma = pltpu.SemaphoreType.DMA
    recv, rfr, rsmall, moments, vmat = pl.pallas_call(
        warp_kernel,
        out_shape=(
            jax.ShapeDtypeStruct((NP, NS, ROWS, S), bf16),
            jax.ShapeDtypeStruct((NP, 16, S), bf16),
            jax.ShapeDtypeStruct((NP, 8, 384), f32),
            jax.ShapeDtypeStruct((16, 128), f32),
            jax.ShapeDtypeStruct((2, 512, 256), bf16),
        ),
        in_specs=[sm, sm, sm, vm, vm, vm, vm, vm, vm, vm],
        out_specs=(hbm, hbm, hbm, vm, vm),
        scratch_shapes=[
            pltpu.VMEM((NS, S, S), bf16),
            pltpu.VMEM((16 * SPILL, S), bf16),
            pltpu.VMEM((896, S), bf16),
            pltpu.VMEM((S, S), bf16),
            pltpu.VMEM((S, S), bf16),
            pltpu.VMEM((NS, 128, S), bf16),
            pltpu.VMEM((2, 128, 256), bf16),
            pltpu.VMEM((8, 2 * S), f32),
            pltpu.VMEM((2, 16, S), f32),
            pltpu.VMEM((128, 384), f32),
            pltpu.VMEM((16, 128), f32),
            pltpu.VMEM((NV, 16, 128), f32),
            dma((NS,)), dma((NS,)),
            dma, dma, dma, dma, dma, dma,
        ],
        compiler_params=pltpu.CompilerParams(
            has_side_effects=True, vmem_limit_bytes=48 * 1024 * 1024
        ),
        name="warp_send",
    )(kern, tile // 2, gain, pix, wts, ylines, outer, outer_x, pp, extra)

    codes = rsmall[:, :, 256].reshape(NP * NS).astype(jnp.int32)
    slab, spill = pl.pallas_call(
        layer_kernel,
        out_shape=(
            jax.ShapeDtypeStruct((2, 64, ROWS, 256), bf16),
            jax.ShapeDtypeStruct((512, 256), bf16),
        ),
        in_specs=[sm, vm, hbm, vm],
        out_specs=(vm, vm),
        scratch_shapes=[
            pltpu.VMEM((2, 2, 66, ROWS, 256), f32),
            pltpu.VMEM((2, 66, 8, 256), f32),
            pltpu.VMEM((NP, 16, S), bf16),
            dma,
        ],
        compiler_params=pltpu.CompilerParams(vmem_limit_bytes=48 * 1024 * 1024),
        name="layer_smooth",
    )(codes, recv, rfr, vmat)

    covers = rsmall[:, :, 0:256].reshape(2 * NP, 2 * S)
    tiles = rsmall[:, ::4, 257].reshape(1, 2 * NP, 1, 1).astype(jnp.int32)
    owner = jnp.arange(NV)[:, None, None, None]
    keep = (tiles // 2 == owner // 4) & (tiles % 2 == jnp.arange(2)[None, None, :, None])
    row_part = covers[:, :S].reshape(2 * NP, 4, 128).transpose(1, 0, 2)
    row_part = jnp.concatenate([row_part, row_part], axis=0)
    row_part = jnp.where(keep, row_part[:, :, None, :], 0.0).reshape(NV, 2 * NP, 256)
    col_part = jnp.broadcast_to(covers[None, :, S:], (NV, 2 * NP, S))
    wmsg = jnp.concatenate([col_part, row_part], axis=2).astype(bf16)

    flux, weight = pl.pallas_call(
        owner_kernel,
        out_shape=(
            jax.ShapeDtypeStruct((128, 2 * S), f32),
            jax.ShapeDtypeStruct((128, 2 * S), f32),
        ),
        in_specs=[vm, vm, vm],
        out_specs=(vm, vm),
        scratch_shapes=[
            pltpu.VMEM((2, NV, 8, ROWS, 256), bf16),
            pltpu.VMEM((2, 8, ROWS, 256), bf16),
            pltpu.VMEM((4, 4, ROWS, 256), bf16),
            pltpu.VMEM((NV, 2 * NP, 768), bf16),
            pltpu.VMEM((NV, 64, 256), bf16),
            pltpu.VMEM((64, 256), f32),
            pltpu.VMEM((SPILL, 32, 256), f32),
            dma((2,)), dma((2,)), dma((2, 2)), dma, dma, dma,
            dma, dma, dma((2, 2)), dma,
        ],
        compiler_params=pltpu.CompilerParams(
            has_side_effects=True, vmem_limit_bytes=48 * 1024 * 1024
        ),
        name="owner_sum",
    )(slab, spill, wmsg)

    norm_factor = 1.0 / (NV * 2 * 4 * S * S)
    first = np.array([pair[0] for pair in PAIRS])
    second = np.array([pair[1] for pair in PAIRS])
    pick_row = np.zeros((100, 16), np.float32)
    pick_col = np.zeros((100, 16), np.float32)
    for q in range(10):
        for r in range(10):
            pick_row[10 * q + r, 4 * first[q] + first[r]] = 1
            pick_col[10 * q + r, 4 * second[q] + second[r]] = 1
    picked = jnp.dot(pick_row, moments[:, :16], precision=precise)
    hessian = jnp.sum(picked * pick_col, axis=1).reshape(1, 10, 10) * norm_factor
    return flux, weight, hessian


def solution(mesh):
    in_specs = (
        P("patch", "visit", None, None, None),
        P("patch", "visit", None, None),
        P("patch", "visit", None, None),
        P("patch", "visit", None),
        P("patch", "visit", None),
        P("patch", "visit", None, None),
        P("patch", "visit", None, None),
        P("patch", "visit", None),
        P("patch", "visit", None),
        P("visit", None, None),
    )
    out_specs = (P("visit", "patch"), P("visit", "patch"), P("patch", None, None))
    return jax.shard_map(body, mesh=mesh, in_specs=in_specs, out_specs=out_specs, check_vma=False)
```

```python
import jax
import jax.numpy as jnp
import numpy as np
from jax import lax
from jax.experimental import pallas as pl
from jax.experimental.pallas import tpu as pltpu
from jax.sharding import PartitionSpec as P

PAIRS = ((0, 0), (1, 0), (0, 1), (2, 0), (1, 1), (0, 2), (3, 0), (2, 1), (1, 2), (0, 3))
MESH = pl.DeviceIdType.MESH
precise = lax.Precision.HIGHEST
f32 = jnp.float32
bf16 = jnp.bfloat16
S = 512
TAPS = 41
NP = 16
NV = 8
NS = 8
ROWS = S // NP
SPILL = 10


def lanczos(offset):
    wide = offset * np.float32(np.pi)
    narrow = wide * np.float32(1.0 / 3.0)
    product = wide * narrow
    ratio = jnp.sin(wide) * jnp.sin(narrow) / jnp.where(product == 0.0, 1.0, product)
    value = jnp.where(product == 0.0, 1.0, ratio)
    return jnp.where(jnp.abs(offset) < 3.0, value, 0.0)


def outer_tables():
    grid_pos = np.arange(S, dtype=np.float32)
    block = np.arange(2, dtype=np.float32)
    coord = (block[:, None] * np.float32(S) + grid_pos[None, :] + np.float32(0.5)) / np.float32(
        S
    ) - np.float32(1.0)
    square = coord * coord
    poly = np.stack(
        [
            np.ones_like(coord),
            coord,
            np.float32(1.5) * square - np.float32(0.5),
            (np.float32(2.5) * square - np.float32(1.5)) * coord,
        ],
        axis=1,
    )
    return (poly[:, :, None, :] * poly[:, None, :, :]).reshape(2, 16, S).astype(bf16)


def dot(a, b, precision=None):
    return jnp.dot(a, b, preferred_element_type=f32, precision=precision)


def dot_nt(a, b, precision=None):
    return lax.dot_general(
        a, b, (((1,), (1,)), ((), ())), preferred_element_type=f32, precision=precision
    )


def dot_tn(a, b):
    return lax.dot_general(a, b, (((0,), (0,)), ((), ())), preferred_element_type=f32)


def band(position, base, weight_of):
    offset = position - base
    value = jnp.zeros(offset.shape, f32)
    for k in range(6):
        value = jnp.where(offset == float(k), weight_of(k), value)
    return value


def spill_row(row):
    return 2 * (row // 16) + row % 2


def sheared(line, rows):
    return pltpu.roll(
        jnp.broadcast_to(line, (rows, line.shape[1])), 0, 1, stride=1, stride_axis=0
    )


def warp_kernel(
    params, route, tile, pix, row_masks, col_masks, psf, oy, ox,
    recv, rfr, rsmall, hess, vmat,
    sbuf, fbuf, wpad, ybuf, half, edges, umat, cov, rmom, small,
    send_sem, recv_sem, fsend, frecv, ssend, srecv,
):
    me_v = lax.axis_index("visit")
    me = lax.axis_index("patch")
    barrier = pltpu.get_barrier_semaphore()

    def greet(j, carry):
        pl.semaphore_signal(
            barrier, inc=1, device_id={"patch": lax.rem(me + j, NP)}, device_id_type=MESH
        )
        return carry

    lax.fori_loop(1, NP, greet, 0)
    pl.semaphore_wait(barrier, NP - 1)
    wpad[0:192, :] = jnp.zeros((192, S), bf16)
    wpad[704:896, :] = jnp.zeros((192, S), bf16)
    rmom[...] = jnp.zeros_like(rmom)
    tap_lines = []
    for v in range(2):
        lines = psf[v] / jnp.sum(psf[v], axis=1, keepdims=True)
        lines = lines.astype(bf16).astype(f32)
        tap_lines.append(lines)
        umat[v] = sheared(lines[1:2], 128).astype(bf16)

    def stretch(s):
        v = s // 4
        piece = s % 4
        is_low = tile[0, v, piece] < 2
        spot = lax.broadcasted_iota(jnp.int32, (8, S), 1).astype(f32) - 256.0
        tap = lax.broadcasted_iota(jnp.int32, (8, S), 0).astype(f32)

        def weights_along(axis, factor):
            shift = params[0, v, piece, 1 + axis] + params[0, v, piece, 3 + axis]
            source = params[0, v, piece, 0] * spot + (256.0 + shift)
            lowest = jnp.floor(source) - 2.0
            value = (factor * lanczos((lowest + tap) - source)).astype(bf16).astype(f32)
            return jnp.where(tap == 6.0, lowest, value)

        columns = jnp.transpose(weights_along(0, 1.0))
        wt = weights_along(1, params[0, v, piece, 5])
        row_mask = row_masks[0, v, pl.ds(piece, 1), :].astype(f32)
        col_mask = col_masks[0, v, pl.ds(piece, 1), :].astype(f32)
        ones = jnp.ones((8, 384), bf16)
        for a in range(2):
            at = lax.broadcasted_iota(jnp.int32, (256, 384), 1).astype(f32) + float(128 * a)
            cols = columns[256 * a : 256 * a + 256]
            weights = band(at, cols[:, 6:7], lambda k: cols[:, k : k + 1])
            rows_map = (weights * row_mask[:, 128 * a : 128 * a + 384]).astype(bf16)
            part = dot(rows_map, pix[s, 128 * a : 128 * a + 384, :])
            half[256 * a : 256 * a + 256, :] = (part * col_mask).astype(bf16)
            cover = dot_nt(ones, rows_map)
            cov[pl.ds(s, 1), 256 * a : 256 * a + 256] = cover[0:1]
        for b in range(2):
            at = lax.broadcasted_iota(jnp.int32, (384, 256), 0).astype(f32) + float(128 * b)
            lanes = wt[:, 256 * b : 256 * b + 256]
            cols_map = band(at, lanes[6:7], lambda k: lanes[k : k + 1]).astype(bf16)
            part = dot(half[:, 128 * b : 128 * b + 384], cols_map)
            wpad[192:704, 256 * b : 256 * b + 256] = part.astype(bf16)
            mask = jnp.broadcast_to(col_mask[:, 128 * b : 128 * b + 384], (8, 384)).astype(bf16)
            cover = dot(mask, cols_map)
            cov[pl.ds(s, 1), S + 256 * b : S + 256 * b + 256] = cover[0:1]
        for a in range(4):
            ybuf[128 * a : 128 * a + 128, :] = dot(
                umat[v], wpad[128 + 128 * a : 384 + 128 * a, :]
            ).astype(bf16)
        for q in range(NP):
            low = ybuf[ROWS * q : ROWS * (q + 1), :]
            high = ybuf[ROWS * (NP - 1 - q) : ROWS * (NP - q), :]
            sbuf[s, ROWS * q : ROWS * (q + 1), :] = jnp.where(is_low, low, high)
        edges[s, 0:64] = wpad[192:256, :]
        edges[s, 64:128] = wpad[640:704, :]

    turn = 7 * me + 3 * me_v

    def step(s, carry):
        stretch(s)

        def send(j, carry):
            k = lax.rem(me + 1 + lax.rem(turn + j, NP - 1), NP)
            pltpu.make_async_remote_copy(
                src_ref=sbuf.at[s, pl.ds(pl.multiple_of(k * ROWS, ROWS), ROWS)],
                dst_ref=recv.at[me, s],
                send_sem=send_sem.at[s],
                recv_sem=recv_sem.at[s],
                device_id={"patch": k},
                device_id_type=MESH,
            ).start()
            return carry

        lax.fori_loop(0, NP - 1, send, 0)
        pltpu.make_async_copy(
            sbuf.at[s, pl.ds(pl.multiple_of(me * ROWS, ROWS), ROWS)], recv.at[me, s], recv_sem.at[s]
        ).start()
        return carry

    lax.fori_loop(0, NS, step, 0)

    row = lax.broadcasted_iota(jnp.int32, (16 * SPILL, 128), 0)
    lane = lax.broadcasted_iota(jnp.int32, (16 * SPILL, 128), 1)
    spilled = jnp.zeros((16 * SPILL, S), f32)
    step_row = spill_row(lax.broadcasted_iota(jnp.int32, (16 * SPILL, 32), 0))
    step_lane = lax.broadcasted_iota(jnp.int32, (16 * SPILL, 32), 1)
    forward = jnp.where(step_lane == step_row, 1.0, 0.0).astype(bf16)
    backward = jnp.where(step_lane == 31 - step_row, 1.0, 0.0).astype(bf16)
    for v in range(2):
        wide = jnp.concatenate([tap_lines[v][1:2], jnp.zeros((1, 256), f32)], axis=1)
        below = sheared(pltpu.roll(wide, 64, 1), 32)[:, 0:128].astype(bf16)
        above = sheared(pltpu.roll(wide, 416, 1), 32)[:, 0:128].astype(bf16)
        taps = jnp.where(lane >= 64, dot(forward, below), dot(backward, above))
        for s in range(4 * v, 4 * v + 4):
            keep = (row % 16 // 2 == s) & (lane // 64 == 1 - tile[0, v, s - 4 * v] // 2)
            spilled += dot(jnp.where(keep, taps, 0.0).astype(bf16), edges[s])
    fbuf[...] = spilled.astype(bf16)

    def send_spill(k, carry):
        src = fbuf.at[pl.ds(pl.multiple_of(16 * k, 16), 16)]

        @pl.when(me != k)
        def _():
            pltpu.make_async_remote_copy(
                src_ref=src,
                dst_ref=rfr.at[me],
                send_sem=fsend,
                recv_sem=frecv,
                device_id={"patch": k},
                device_id_type=MESH,
            ).start()

        @pl.when(me == k)
        def _():
            pltpu.make_async_copy(src, rfr.at[me], frecv).start()

        return carry

    lax.fori_loop(0, SPILL, send_spill, 0)

    def moments(s, carry):
        piece = s % 4
        values = pix[s].astype(f32)
        square = (values * values).astype(bf16)
        v = s // 4
        lhs = oy[piece // 2] * row_masks[0, v, pl.ds(piece, 1), :].astype(f32).astype(bf16)
        col_mask = col_masks[0, v, pl.ds(piece, 1), :].astype(f32)
        rmom[piece % 2] += dot(lhs, square) * (col_mask * params[0, v, piece, 5])
        return carry

    lax.fori_loop(0, NS, moments, 0)
    row = lax.broadcasted_iota(jnp.int32, (8 * NP, 256), 0)
    slots = jnp.zeros((8 * NP, 256), f32)
    line = lax.broadcasted_iota(jnp.int32, (8 * NP, 128), 0)
    codes = jnp.zeros((8 * NP, 128), f32)
    slot_tile = jnp.zeros((8 * NP, 128), f32)
    routes = [route[0, s // 4, s % 4] for s in range(NS)]
    for s in range(NS):
        rank = jnp.int32(0)
        for before in range(s):
            rank += (routes[before] == routes[s]).astype(jnp.int32)
        cover = cov[s : s + 1].astype(bf16).astype(f32)
        values = cover[:, 0:256]
        for b in range(1, 4):
            values = jnp.where(row % 4 == b, cover[:, 256 * b : 256 * b + 256], values)
        slots += jnp.where((row // 8 == routes[s]) & (row % 8 // 4 == rank), values, 0.0)
        mine = tile[0, s // 4, s % 4]
        codes = jnp.where(line % 8 == s, (4 * routes[s] + mine).astype(f32), codes)
        slot_tile = jnp.where(
            (line // 8 == routes[s]) & (line % 8 // 4 == rank), mine.astype(f32), slot_tile
        )
    small[:, 0:256] = slots
    lane = lax.broadcasted_iota(jnp.int32, (8 * NP, 128), 1)
    small[:, 256:384] = jnp.where(lane == 0, codes, slot_tile)
    hess[...] = dot_nt(rmom[0], ox[0], precise) + dot_nt(rmom[1], ox[1], precise)

    def send_small(j, carry):
        k = lax.rem(me + j, NP)
        pltpu.make_async_remote_copy(
            src_ref=small.at[pl.ds(pl.multiple_of(k * 8, 8), 8)],
            dst_ref=rsmall.at[me],
            send_sem=ssend,
            recv_sem=srecv,
            device_id={"patch": k},
            device_id_type=MESH,
        ).start()
        return carry

    lax.fori_loop(1, NP, send_small, 0)
    pltpu.make_async_copy(
        small.at[pl.ds(pl.multiple_of(me * 8, 8), 8)], rsmall.at[me], srecv
    ).start()

    for v in range(2):
        wide = jnp.concatenate([tap_lines[v][0:1], jnp.zeros((1, 256), f32)], axis=1)
        for c in range(2):
            part = sheared(pltpu.roll(wide, 64 + 128 * c, 1), 128)
            vmat[v, :, 128 * c : 128 * c + 128] = jnp.transpose(part).astype(bf16)

    pltpu.make_async_copy(rsmall, rsmall, srecv).wait()
    pltpu.make_async_copy(rsmall.at[1:NP], rsmall.at[1:NP], ssend).wait()

    def finish(i, carry):
        everyone = recv.at[:, i]
        others = recv.at[1:NP, i]
        pltpu.make_async_copy(everyone, everyone, recv_sem.at[i]).wait()
        pltpu.make_async_copy(others, others, send_sem.at[i]).wait()
        return carry

    lax.fori_loop(0, NS, finish, 0)

    @pl.when(me < SPILL)
    def _():
        others = fbuf.at[0 : 16 * (SPILL - 1)]
        pltpu.make_async_copy(rfr, rfr, frecv).wait()
        pltpu.make_async_copy(others, others, fsend).wait()

    @pl.when(me >= SPILL)
    def _():
        pltpu.make_async_copy(fbuf, fbuf, fsend).wait()


def layer_kernel(codes, recv, rfr, vmat, out, outf, acc, accf, fvm, sem):
    me = lax.axis_index("patch")
    zero = jnp.zeros((ROWS, 256), f32)

    def clear(b, carry):
        for v in range(2):
            for t in range(2):
                acc[v, t, b] = zero
        return carry

    lax.fori_loop(0, 66, clear, 0)

    def add(at, carry):
        s = at % NS
        code = codes[at]
        tile = code % 4
        g = 2 * (code // 4) + tile % 2
        t = tile // 2
        data = recv[at // NS, s].astype(f32)
        acc[s // 4, t, 2 * g + 1] += data[:, 0:256]
        acc[s // 4, t, 2 * g + 2] += data[:, 256:512]
        return carry

    lax.fori_loop(0, NP * NS, add, 0)

    def smooth(blocks_of, count):
        total = None
        rows = blocks_of(0).shape[0] // (count + 2)
        for v in range(2):
            block = blocks_of(v)
            part = dot(block[rows : (count + 1) * rows], vmat[v, 128:384])
            part += dot(block[0 : count * rows, 128:256], vmat[v, 0:128])
            part += dot(block[2 * rows : (count + 2) * rows, 0:128], vmat[v, 384:512])
            total = part if total is None else total + part
        return total

    for t in range(2):
        for c in range(4):
            total = smooth(
                lambda v: acc[v, t, 16 * c : 16 * c + 18].reshape(18 * ROWS, 256).astype(bf16), 16
            )
            out[t, 16 * c : 16 * c + 16] = total.astype(bf16).reshape(16, ROWS, 256)

    @pl.when(me < SPILL)
    def _():
        copy = pltpu.make_async_copy(rfr, fvm, sem)
        copy.start()
        accf[...] = jnp.zeros_like(accf)
        copy.wait()
        target = lax.broadcasted_iota(jnp.int32, (8, S), 0) // 2

        def add_spill(c, carry):
            rows = fvm[c].astype(f32)
            for s in range(NS):
                code = codes[c * NS + s]
                tile = code % 4
                g = 2 * (code // 4) + tile % 2
                two = rows[2 * s : 2 * s + 2]
                data = jnp.where(
                    target == 1 - tile // 2, jnp.concatenate([two, two, two, two], axis=0), 0.0
                )
                accf[s // 4, 2 * g + 1] += data[:, 0:256]
                accf[s // 4, 2 * g + 2] += data[:, 256:512]
            return carry

        lax.fori_loop(0, NP, add_spill, 0)
        blocks = smooth(lambda v: accf[v].reshape(66 * 8, 256).astype(bf16), 64)
        blocks = blocks.reshape(8, 2, 32, 256)
        packed = blocks[:, 0] + pltpu.roll(blocks[:, 1], 4, 1)
        outf[...] = packed.reshape(256, 256).astype(bf16)


def owner_kernel(
    slab, spill, wmsg, moment, pick_row, pick_col, flux, weight, hess,
    part, summed, frecv, wrecv, spart, ssum, srecv,
    part_send, part_recv, sum_send, sum_recv, wsend_sem, wrecv_sem,
    spart_send, spart_recv, ssum_send, ssum_recv, mrecv, msend_sem, mrecv_sem,
):
    me_v = lax.axis_index("visit")
    me = lax.axis_index("patch")

    turn = 3 * me_v + 2 * me

    def group(v):
        return lax.rem(v + me // 2, NV)

    mine_group = group(me_v)
    barrier = pltpu.get_barrier_semaphore()

    def greet(v, p):
        pl.semaphore_signal(
            barrier, inc=1, device_id={"visit": v, "patch": p}, device_id_type=MESH
        )

    def greet_visit(j, carry):
        greet(lax.rem(me_v + j, NV), me)
        return carry

    lax.fori_loop(1, NV, greet_visit, 0)
    upper = me_v // 4

    def sender(k):
        return lax.rem(me // 2 - k // 2 + NV, NV)

    for slot in range(4):
        block = 4 * lax.rem(me_v, 4) + slot
        k = block + upper * (NP - 1 - 2 * block)
        v = sender(k)

        @pl.when(jnp.logical_not((v == me_v) & (k == me)))
        def _():
            greet(v, k)

    @pl.when((me_v == 3) | (me_v == 4))
    def _():
        def greet_spill(k, carry):
            v = sender(k)

            @pl.when(jnp.logical_not((v == me_v) & (k == me)))
            def _():
                greet(v, k)

            return carry

        lax.fori_loop(0, SPILL, greet_spill, 0)

    inside = (me // 2 == mine_group).astype(jnp.int32)
    lower_here = (me_v == me // 4).astype(jnp.int32)
    upper_here = (me_v == 4 + (NP - 1 - me) // 4).astype(jnp.int32)
    edge = ((me_v == 3) | (me_v == 4)).astype(jnp.int32)
    spills = (me < SPILL).astype(jnp.int32)
    pl.semaphore_wait(
        barrier,
        NV - 1 + 4 - inside * (lower_here + upper_here) + spills * (4 - inside * edge),
    )

    def send_moment(j, carry):
        pltpu.make_async_remote_copy(
            src_ref=moment,
            dst_ref=mrecv.at[me_v],
            send_sem=msend_sem,
            recv_sem=mrecv_sem,
            device_id={"visit": lax.rem(me_v + j, NV)},
            device_id_type=MESH,
        ).start()
        return carry


    for t in range(2):

        def send_part(j, carry):
            r = lax.rem(me_v + 1 + lax.rem(turn + j, NV - 1), NV)
            pltpu.make_async_remote_copy(
                src_ref=slab.at[t, pl.ds(8 * group(r), 8)],
                dst_ref=part.at[t, me_v],
                send_sem=part_send.at[t],
                recv_sem=part_recv.at[t],
                device_id={"visit": r},
                device_id_type=MESH,
            ).start()
            return carry

        lax.fori_loop(0, NV - 1, send_part, 0)
        pltpu.make_async_copy(
            slab.at[t, pl.ds(8 * mine_group, 8)], part.at[t, me_v], part_recv.at[t]
        ).start()

    @pl.when(me < SPILL)
    def _():
        def send_spill(j, carry):
            r = lax.rem(me_v + j, NV)
            pltpu.make_async_remote_copy(
                src_ref=spill.at[pl.ds(pl.multiple_of(32 * group(r), 32), 32)],
                dst_ref=spart.at[me_v],
                send_sem=spart_send,
                recv_sem=spart_recv,
                device_id={"visit": r},
                device_id_type=MESH,
            ).start()
            return carry

        lax.fori_loop(1, NV, send_spill, 0)
        pltpu.make_async_copy(
            spill.at[pl.ds(pl.multiple_of(32 * mine_group, 32), 32)], spart.at[me_v], spart_recv
        ).start()

    def send_weight(j, carry):
        r = lax.rem(me_v + j, NV)
        pltpu.make_async_remote_copy(
            src_ref=wmsg.at[r],
            dst_ref=wrecv.at[me_v],
            send_sem=wsend_sem,
            recv_sem=wrecv_sem,
            device_id={"visit": r},
            device_id_type=MESH,
        ).start()
        return carry

    lax.fori_loop(1, NV, send_weight, 0)
    lax.fori_loop(1, NV, send_moment, 0)
    pltpu.make_async_copy(moment, mrecv.at[me_v], mrecv_sem).start()
    pltpu.make_async_copy(wmsg.at[me_v], wrecv.at[me_v], wrecv_sem).start()

    for t in range(2):
        block = me if t == 0 else NP - 1 - me
        r = 4 * t + block // 4
        slot = lax.rem(block, 4)
        pltpu.make_async_copy(part.at[t], part.at[t], part_recv.at[t]).wait()

        def add(b, carry):
            total = part[t, 0, b].astype(f32)
            for v in range(1, NV):
                total += part[t, v, b].astype(f32)
            summed[t, b] = total.astype(bf16)
            return carry

        lax.fori_loop(0, 8, add, 0)
        for half in range(2):
            p = 2 * mine_group + half
            mine = (r == me_v) & (p == me)
            src = summed.at[t, 4 * half : 4 * half + 4]

            @pl.when(jnp.logical_not(mine))
            def _():
                pltpu.make_async_remote_copy(
                    src_ref=src,
                    dst_ref=frecv.at[slot],
                    send_sem=sum_send.at[t, half],
                    recv_sem=sum_recv,
                    device_id={"visit": r, "patch": p},
                    device_id_type=MESH,
                ).start()

            @pl.when(mine)
            def _():
                pltpu.make_async_copy(src, frecv.at[slot], sum_recv).start()

    def spill_legs(act):
        for half in range(2):
            for t in range(2):
                act(half, t, (me_v == 3 + t) & (me == 2 * mine_group + half))

    @pl.when(me < SPILL)
    def _():
        pltpu.make_async_copy(spart, spart, spart_recv).wait()
        total = spart[0].astype(f32)
        for v in range(1, NV):
            total += spart[v].astype(f32)
        ssum[...] = total.astype(bf16)

        def leg(half, t, mine):
            src = ssum

            @pl.when(jnp.logical_not(mine))
            def _():
                pltpu.make_async_remote_copy(
                    src_ref=src,
                    dst_ref=srecv.at[me],
                    send_sem=ssum_send.at[t, half],
                    recv_sem=ssum_recv,
                    device_id={"visit": 3 + t, "patch": 2 * mine_group + half},
                    device_id_type=MESH,
                ).start()

            @pl.when(mine)
            def _():
                pltpu.make_async_copy(src, srecv.at[me], ssum_recv).start()

        spill_legs(leg)

    pltpu.make_async_copy(wrecv, wrecv, wrecv_sem).wait()
    cols = wrecv[:, :, 0:512].reshape(NV * 2 * NP, 512)
    left = wrecv[:, :, 512:640].reshape(NV * 2 * NP, 128)
    right = wrecv[:, :, 640:768].reshape(NV * 2 * NP, 128)
    weight[:, 0:512] = dot_tn(left, cols)
    weight[:, 512:1024] = dot_tn(right, cols)
    pltpu.make_async_copy(mrecv, mrecv, mrecv_sem).wait()
    total = mrecv[0]
    for v in range(1, NV):
        total += mrecv[v]
    picked = dot(pick_row[...], total, precise) * pick_col[...]
    sums = jnp.sum(picked, axis=1, keepdims=True)
    lane = lax.broadcasted_iota(jnp.int32, (16, 128), 1)
    matrix = jnp.zeros((16, 128), f32)
    for q in range(10):
        matrix = jnp.where(lane == q, sums[16 * q : 16 * q + 16], matrix)
    hess[0] = matrix[0:10, 0:10] * (1.0 / (NV * 2 * 4 * S * S))
    pltpu.make_async_copy(mrecv.at[1:NV], mrecv.at[1:NV], msend_sem).wait()
    pltpu.make_async_copy(frecv, frecv, sum_recv).wait()
    for slot in range(4):
        for q in range(4):
            flux[32 * slot : 32 * slot + 32, 256 * q : 256 * q + 256] = frecv[slot, q].astype(f32)
    for t in range(2):

        @pl.when(me_v == 3 + t)
        def _():
            pltpu.make_async_copy(srecv, srecv, ssum_recv).wait()
            odd = lax.rem(me, 2) == 1
            for k in range(SPILL):
                got = srecv[k].astype(f32)
                rows8 = [
                    jnp.where(odd, got[8 * q + 4 : 8 * q + 8], got[8 * q : 8 * q + 4])
                    for q in range(4)
                ]
                for e in range(2):
                    at = 2 * k + e
                    line = at if t == 1 else 127 - at
                    for q in range(4):
                        flux[line : line + 1, 256 * q : 256 * q + 256] += rows8[q][
                            2 * t + e : 2 * t + e + 1
                        ]

    @pl.when(me < SPILL)
    def _():
        pltpu.make_async_copy(spart.at[1:NV], spart.at[1:NV], spart_send).wait()

        def leg_sent(half, t, mine):
            @pl.when(jnp.logical_not(mine))
            def _():
                src = ssum
                pltpu.make_async_copy(src, src, ssum_send.at[t, half]).wait()

        spill_legs(leg_sent)

    pltpu.make_async_copy(wrecv.at[1:NV], wrecv.at[1:NV], wsend_sem).wait()
    for t in range(2):
        block = me if t == 0 else NP - 1 - me
        r = 4 * t + block // 4
        pltpu.make_async_copy(part.at[t, 1:NV], part.at[t, 1:NV], part_send.at[t]).wait()
        for half in range(2):
            mine = (r == me_v) & (2 * mine_group + half == me)

            @pl.when(jnp.logical_not(mine))
            def _():
                src = summed.at[t, 4 * half : 4 * half + 4]
                pltpu.make_async_copy(src, src, sum_send.at[t, half]).wait()


def body(
    pixels, row_mask, col_mask, route, tile, wcs_offset, subpixel, plate_scale, stretch_weight, psf_taps
):
    pix = pixels.reshape(NS, S, S)
    params = jnp.concatenate(
        [
            plate_scale[..., None].astype(f32),
            wcs_offset.astype(f32),
            subpixel.astype(f32),
            stretch_weight[..., None].astype(f32),
        ],
        axis=-1,
    )
    psf = jnp.pad(psf_taps, ((0, 0), (0, 0), (44, 256 - 44 - TAPS)))
    outer = outer_tables()
    outer_x = np.pad(outer.astype(np.float32), ((0, 0), (0, 112), (0, 0)))
    vm = pl.BlockSpec(memory_space=pltpu.VMEM)
    sm = pl.BlockSpec(memory_space=pltpu.SMEM)
    hbm = pl.BlockSpec(memory_space=pl.ANY)
    dma = pltpu.SemaphoreType.DMA
    recv, rfr, rsmall, moments, vmat = pl.pallas_call(
        warp_kernel,
        out_shape=(
            jax.ShapeDtypeStruct((NP, NS, ROWS, S), bf16),
            jax.ShapeDtypeStruct((NP, 16, S), bf16),
            jax.ShapeDtypeStruct((NP, 8, 384), f32),
            jax.ShapeDtypeStruct((16, 128), f32),
            jax.ShapeDtypeStruct((2, 512, 256), bf16),
        ),
        in_specs=[sm, sm, sm, vm, vm, vm, vm, vm, vm],
        out_specs=(hbm, hbm, hbm, vm, vm),
        scratch_shapes=[
            pltpu.VMEM((NS, S, S), bf16),
            pltpu.VMEM((16 * SPILL, S), bf16),
            pltpu.VMEM((896, S), bf16),
            pltpu.VMEM((S, S), bf16),
            pltpu.VMEM((S, S), bf16),
            pltpu.VMEM((NS, 128, S), bf16),
            pltpu.VMEM((2, 128, 256), bf16),
            pltpu.VMEM((8, 2 * S), f32),
            pltpu.VMEM((2, 16, S), f32),
            pltpu.VMEM((128, 384), f32),
            dma((NS,)), dma((NS,)),
            dma, dma, dma, dma,
        ],
        compiler_params=pltpu.CompilerParams(
            has_side_effects=True, vmem_limit_bytes=60 * 1024 * 1024, collective_id=1
        ),
        name="warp_send",
    )(params, route, tile, pix, row_mask, col_mask, psf, outer, outer_x)

    codes = rsmall[:, :, 256].reshape(NP * NS).astype(jnp.int32)
    slab, spill = pl.pallas_call(
        layer_kernel,
        out_shape=(
            jax.ShapeDtypeStruct((2, 64, ROWS, 256), bf16),
            jax.ShapeDtypeStruct((256, 256), bf16),
        ),
        in_specs=[sm, vm, hbm, vm],
        out_specs=(vm, vm),
        scratch_shapes=[
            pltpu.VMEM((2, 2, 66, ROWS, 256), f32),
            pltpu.VMEM((2, 66, 8, 256), f32),
            pltpu.VMEM((NP, 16, S), bf16),
            dma,
        ],
        compiler_params=pltpu.CompilerParams(vmem_limit_bytes=48 * 1024 * 1024),
        name="layer_smooth",
    )(codes, recv, rfr, vmat)

    covers = rsmall[:, :, 0:256].reshape(2 * NP, 2 * S)
    tiles = rsmall[:, ::4, 257].reshape(1, 2 * NP, 1, 1).astype(jnp.int32)
    owner = jnp.arange(NV)[:, None, None, None]
    keep = (tiles // 2 == owner // 4) & (tiles % 2 == jnp.arange(2)[None, None, :, None])
    row_part = covers[:, :S].reshape(2 * NP, 4, 128).transpose(1, 0, 2)
    row_part = jnp.concatenate([row_part, row_part], axis=0)
    row_part = jnp.where(keep, row_part[:, :, None, :], 0.0).reshape(NV, 2 * NP, 256)
    col_part = jnp.broadcast_to(covers[None, :, S:], (NV, 2 * NP, S))
    wmsg = jnp.concatenate([col_part, row_part], axis=2).astype(bf16)

    pick_row = np.zeros((160, 16), np.float32)
    pick_col = np.zeros((160, 128), np.float32)
    for q in range(10):
        for r in range(10):
            pick_row[16 * q + r, 4 * PAIRS[q][0] + PAIRS[r][0]] = 1
            pick_col[16 * q + r, 4 * PAIRS[q][1] + PAIRS[r][1]] = 1
    flux, weight, hessian = pl.pallas_call(
        owner_kernel,
        out_shape=(
            jax.ShapeDtypeStruct((128, 2 * S), f32),
            jax.ShapeDtypeStruct((128, 2 * S), f32),
            jax.ShapeDtypeStruct((1, 10, 10), f32),
        ),
        in_specs=[vm, vm, vm, vm, vm, vm],
        out_specs=(vm, vm, vm),
        scratch_shapes=[
            pltpu.VMEM((2, NV, 8, ROWS, 256), bf16),
            pltpu.VMEM((2, 8, ROWS, 256), bf16),
            pltpu.VMEM((4, 4, ROWS, 256), bf16),
            pltpu.VMEM((NV, 2 * NP, 768), bf16),
            pltpu.VMEM((NV, 32, 256), bf16),
            pltpu.VMEM((32, 256), bf16),
            pltpu.VMEM((SPILL, 32, 256), bf16),
            dma((2,)), dma((2,)), dma((2, 2)), dma, dma, dma,
            dma, dma, dma((2, 2)), dma,
            pltpu.VMEM((NV, 16, 128), f32),
            dma, dma,
        ],
        compiler_params=pltpu.CompilerParams(
            has_side_effects=True, vmem_limit_bytes=48 * 1024 * 1024, collective_id=2
        ),
        name="owner_sum",
    )(slab, spill, wmsg, moments, pick_row, pick_col)

    return flux, weight, hessian


def solution(mesh):
    in_specs = (
        P("patch", "visit", None, None, None),
        P("patch", "visit", None, None),
        P("patch", "visit", None, None),
        P("patch", "visit", None),
        P("patch", "visit", None),
        P("patch", "visit", None, None),
        P("patch", "visit", None, None),
        P("patch", "visit", None),
        P("patch", "visit", None),
        P("visit", None, None),
    )
    out_specs = (P("visit", "patch"), P("visit", "patch"), P("patch", None, None))
    return jax.shard_map(body, mesh=mesh, in_specs=in_specs, out_specs=out_specs, check_vma=False)
```

```python
import jax
import jax.numpy as jnp
import numpy as np
from jax import lax
from jax.experimental import pallas as pl
from jax.experimental.pallas import tpu as pltpu
from jax.sharding import PartitionSpec as P

PAIRS = ((0, 0), (1, 0), (0, 1), (2, 0), (1, 1), (0, 2), (3, 0), (2, 1), (1, 2), (0, 3))
MESH = pl.DeviceIdType.MESH
precise = lax.Precision.HIGHEST
f32 = jnp.float32
bf16 = jnp.bfloat16
S = 512
TAPS = 41
NP = 16
NV = 8
NS = 8
ROWS = S // NP
SPILL = 10


def lanczos(offset):
    wide = offset * np.float32(np.pi)
    narrow = wide * np.float32(1.0 / 3.0)
    product = wide * narrow
    ratio = jnp.sin(wide) * jnp.sin(narrow) / jnp.where(product == 0.0, 1.0, product)
    value = jnp.where(product == 0.0, 1.0, ratio)
    return jnp.where(jnp.abs(offset) < 3.0, value, 0.0)


def outer_tables():
    grid_pos = np.arange(S, dtype=np.float32)
    block = np.arange(2, dtype=np.float32)
    coord = (block[:, None] * np.float32(S) + grid_pos[None, :] + np.float32(0.5)) / np.float32(
        S
    ) - np.float32(1.0)
    square = coord * coord
    poly = np.stack(
        [
            np.ones_like(coord),
            coord,
            np.float32(1.5) * square - np.float32(0.5),
            (np.float32(2.5) * square - np.float32(1.5)) * coord,
        ],
        axis=1,
    )
    return (poly[:, :, None, :] * poly[:, None, :, :]).reshape(2, 16, S).astype(bf16)


def dot(a, b, precision=None):
    return jnp.dot(a, b, preferred_element_type=f32, precision=precision)


def dot_nt(a, b, precision=None):
    return lax.dot_general(
        a, b, (((1,), (1,)), ((), ())), preferred_element_type=f32, precision=precision
    )


def dot_tn(a, b):
    return lax.dot_general(a, b, (((0,), (0,)), ((), ())), preferred_element_type=f32)


def band(position, base, weight_of):
    offset = position - base
    value = jnp.zeros(offset.shape, f32)
    for k in range(6):
        value = jnp.where(offset == float(k), weight_of(k), value)
    return value


def spill_row(row):
    return 2 * (row // 16) + row % 2


def sheared(line, rows):
    return pltpu.roll(
        jnp.broadcast_to(line, (rows, line.shape[1])), 0, 1, stride=1, stride_axis=0
    )


def warp_kernel(
    params, route, tile, pixels, row_masks, col_masks, psf, oy, ox,
    recv, rfr, rsmall, hess, vmat,
    pix, lines, sbuf, fbuf, wpad, ybuf, half, edges, umat, cov, rmom, small,
    pix_sem, send_sem, recv_sem, fsend, frecv, ssend, srecv,
):
    me_v = lax.axis_index("visit")
    me = lax.axis_index("patch")
    barrier = pltpu.get_barrier_semaphore()

    def greet(j, carry):
        pl.semaphore_signal(
            barrier, inc=1, device_id={"patch": lax.rem(me + j, NP)}, device_id_type=MESH
        )
        return carry

    lax.fori_loop(1, NP, greet, 0)

    def pixel_copy(s):
        return pltpu.make_async_copy(pixels.at[s], pix.at[s], pix_sem.at[s])

    for s in range(NS):
        pixel_copy(s).start()
    lines[...] = jnp.zeros_like(lines)
    wpad[0:192, :] = jnp.zeros((192, S), bf16)
    wpad[704:896, :] = jnp.zeros((192, S), bf16)
    rmom[...] = jnp.zeros_like(rmom)
    tap_lines = []
    for v in range(2):
        kernels = psf[v] / jnp.sum(psf[v], axis=1, keepdims=True)
        lines[2 * v : 2 * v + 2, 0:TAPS] = kernels.astype(bf16).astype(f32)
        placed = pltpu.roll(lines[...], 44, 1)
        tap_lines.append(placed[2 * v : 2 * v + 2])
        umat[v] = sheared(placed[2 * v + 1 : 2 * v + 2], 128).astype(bf16)

    def stretch(s):
        v = s // 4
        piece = s % 4
        is_low = tile[0, v, piece] < 2
        spot = lax.broadcasted_iota(jnp.int32, (8, S), 1).astype(f32) - 256.0
        tap = lax.broadcasted_iota(jnp.int32, (8, S), 0).astype(f32)

        def weights_along(axis, factor):
            shift = params[0, v, piece, 1 + axis] + params[0, v, piece, 3 + axis]
            source = params[0, v, piece, 0] * spot + (256.0 + shift)
            lowest = jnp.floor(source) - 2.0
            value = (factor * lanczos((lowest + tap) - source)).astype(bf16).astype(f32)
            return jnp.where(tap == 6.0, lowest, value)

        columns = jnp.transpose(weights_along(0, 1.0))
        pixel_copy(s).wait()
        wt = weights_along(1, params[0, v, piece, 5])
        row_mask = row_masks[0, v, pl.ds(piece, 1), :].astype(f32)
        col_mask = col_masks[0, v, pl.ds(piece, 1), :].astype(f32)
        ones = jnp.ones((8, 384), bf16)
        for a in range(2):
            at = lax.broadcasted_iota(jnp.int32, (256, 384), 1).astype(f32) + float(128 * a)
            cols = columns[256 * a : 256 * a + 256]
            weights = band(at, cols[:, 6:7], lambda k: cols[:, k : k + 1])
            rows_map = (weights * row_mask[:, 128 * a : 128 * a + 384]).astype(bf16)
            part = dot(rows_map, pix[s, 128 * a : 128 * a + 384, :])
            half[256 * a : 256 * a + 256, :] = (part * col_mask).astype(bf16)
            cover = dot_nt(ones, rows_map)
            cov[pl.ds(s, 1), 256 * a : 256 * a + 256] = cover[0:1]
        for b in range(2):
            at = lax.broadcasted_iota(jnp.int32, (384, 256), 0).astype(f32) + float(128 * b)
            lanes = wt[:, 256 * b : 256 * b + 256]
            cols_map = band(at, lanes[6:7], lambda k: lanes[k : k + 1]).astype(bf16)
            part = dot(half[:, 128 * b : 128 * b + 384], cols_map)
            wpad[192:704, 256 * b : 256 * b + 256] = part.astype(bf16)
            mask = jnp.broadcast_to(col_mask[:, 128 * b : 128 * b + 384], (8, 384)).astype(bf16)
            cover = dot(mask, cols_map)
            cov[pl.ds(s, 1), S + 256 * b : S + 256 * b + 256] = cover[0:1]
        for a in range(4):
            ybuf[128 * a : 128 * a + 128, :] = dot(
                umat[v], wpad[128 + 128 * a : 384 + 128 * a, :]
            ).astype(bf16)
        for q in range(NP):
            low = ybuf[ROWS * q : ROWS * (q + 1), :]
            high = ybuf[ROWS * (NP - 1 - q) : ROWS * (NP - q), :]
            sbuf[s, ROWS * q : ROWS * (q + 1), :] = jnp.where(is_low, low, high)
        edges[s, 0:64] = wpad[192:256, :]
        edges[s, 64:128] = wpad[640:704, :]

    turn = 7 * me + 3 * me_v

    def send_slabs(s):
        def send(j, carry):
            k = lax.rem(me + 1 + lax.rem(turn + j, NP - 1), NP)
            pltpu.make_async_remote_copy(
                src_ref=sbuf.at[s, pl.ds(pl.multiple_of(k * ROWS, ROWS), ROWS)],
                dst_ref=recv.at[me, s],
                send_sem=send_sem.at[s],
                recv_sem=recv_sem.at[s],
                device_id={"patch": k},
                device_id_type=MESH,
            ).start()
            return carry

        lax.fori_loop(0, NP - 1, send, 0)
        pltpu.make_async_copy(
            sbuf.at[s, pl.ds(pl.multiple_of(me * ROWS, ROWS), ROWS)], recv.at[me, s], recv_sem.at[s]
        ).start()

    stretch(0)
    pl.semaphore_wait(barrier, NP - 1)

    def step(s, carry):
        send_slabs(s)
        stretch(s + 1)
        return carry

    lax.fori_loop(0, NS - 1, step, 0)
    send_slabs(NS - 1)

    row = lax.broadcasted_iota(jnp.int32, (16 * SPILL, 128), 0)
    lane = lax.broadcasted_iota(jnp.int32, (16 * SPILL, 128), 1)
    spilled = jnp.zeros((16 * SPILL, S), f32)
    step_row = spill_row(lax.broadcasted_iota(jnp.int32, (16 * SPILL, 32), 0))
    step_lane = lax.broadcasted_iota(jnp.int32, (16 * SPILL, 32), 1)
    forward = jnp.where(step_lane == step_row, 1.0, 0.0).astype(bf16)
    backward = jnp.where(step_lane == 31 - step_row, 1.0, 0.0).astype(bf16)
    for v in range(2):
        wide = jnp.concatenate([tap_lines[v][1:2], jnp.zeros((1, 256), f32)], axis=1)
        below = sheared(pltpu.roll(wide, 64, 1), 32)[:, 0:128].astype(bf16)
        above = sheared(pltpu.roll(wide, 416, 1), 32)[:, 0:128].astype(bf16)
        taps = jnp.where(lane >= 64, dot(forward, below), dot(backward, above))
        for s in range(4 * v, 4 * v + 4):
            keep = (row % 16 // 2 == s) & (lane // 64 == 1 - tile[0, v, s - 4 * v] // 2)
            spilled += dot(jnp.where(keep, taps, 0.0).astype(bf16), edges[s])
    fbuf[...] = spilled.astype(bf16)

    def send_spill(k, carry):
        src = fbuf.at[pl.ds(pl.multiple_of(16 * k, 16), 16)]

        @pl.when(me != k)
        def _():
            pltpu.make_async_remote_copy(
                src_ref=src,
                dst_ref=rfr.at[me],
                send_sem=fsend,
                recv_sem=frecv,
                device_id={"patch": k},
                device_id_type=MESH,
            ).start()

        @pl.when(me == k)
        def _():
            pltpu.make_async_copy(src, rfr.at[me], frecv).start()

        return carry

    lax.fori_loop(0, SPILL, send_spill, 0)

    def moments(s, carry):
        piece = s % 4
        values = pix[s].astype(f32)
        square = (values * values).astype(bf16)
        v = s // 4
        lhs = oy[piece // 2] * row_masks[0, v, pl.ds(piece, 1), :].astype(f32).astype(bf16)
        col_mask = col_masks[0, v, pl.ds(piece, 1), :].astype(f32)
        rmom[piece % 2] += dot(lhs, square) * (col_mask * params[0, v, piece, 5])
        return carry

    lax.fori_loop(0, NS, moments, 0)
    row = lax.broadcasted_iota(jnp.int32, (8 * NP, 256), 0)
    slots = jnp.zeros((8 * NP, 256), f32)
    line = lax.broadcasted_iota(jnp.int32, (8 * NP, 128), 0)
    codes = jnp.zeros((8 * NP, 128), f32)
    slot_tile = jnp.zeros((8 * NP, 128), f32)
    routes = [route[0, s // 4, s % 4] for s in range(NS)]
    for s in range(NS):
        rank = jnp.int32(0)
        for before in range(s):
            rank += (routes[before] == routes[s]).astype(jnp.int32)
        cover = cov[s : s + 1].astype(bf16).astype(f32)
        values = cover[:, 0:256]
        for b in range(1, 4):
            values = jnp.where(row % 4 == b, cover[:, 256 * b : 256 * b + 256], values)
        slots += jnp.where((row // 8 == routes[s]) & (row % 8 // 4 == rank), values, 0.0)
        mine = tile[0, s // 4, s % 4]
        codes = jnp.where(line % 8 == s, (4 * routes[s] + mine).astype(f32), codes)
        slot_tile = jnp.where(
            (line // 8 == routes[s]) & (line % 8 // 4 == rank), mine.astype(f32), slot_tile
        )
    small[:, 0:256] = slots
    lane = lax.broadcasted_iota(jnp.int32, (8 * NP, 128), 1)
    small[:, 256:384] = jnp.where(lane == 0, codes, slot_tile)
    hess[...] = dot_nt(rmom[0], ox[0], precise) + dot_nt(rmom[1], ox[1], precise)

    def send_small(j, carry):
        k = lax.rem(me + j, NP)
        pltpu.make_async_remote_copy(
            src_ref=small.at[pl.ds(pl.multiple_of(k * 8, 8), 8)],
            dst_ref=rsmall.at[me],
            send_sem=ssend,
            recv_sem=srecv,
            device_id={"patch": k},
            device_id_type=MESH,
        ).start()
        return carry

    lax.fori_loop(1, NP, send_small, 0)
    pltpu.make_async_copy(
        small.at[pl.ds(pl.multiple_of(me * 8, 8), 8)], rsmall.at[me], srecv
    ).start()

    for v in range(2):
        wide = jnp.concatenate([tap_lines[v][0:1], jnp.zeros((1, 256), f32)], axis=1)
        for c in range(2):
            part = sheared(pltpu.roll(wide, 64 + 128 * c, 1), 128)
            vmat[v, :, 128 * c : 128 * c + 128] = jnp.transpose(part).astype(bf16)

    pltpu.make_async_copy(rsmall, rsmall, srecv).wait()
    pltpu.make_async_copy(rsmall.at[1:NP], rsmall.at[1:NP], ssend).wait()

    def finish(i, carry):
        everyone = recv.at[:, i]
        others = recv.at[1:NP, i]
        pltpu.make_async_copy(everyone, everyone, recv_sem.at[i]).wait()
        pltpu.make_async_copy(others, others, send_sem.at[i]).wait()
        return carry

    lax.fori_loop(0, NS, finish, 0)

    @pl.when(me < SPILL)
    def _():
        others = fbuf.at[0 : 16 * (SPILL - 1)]
        pltpu.make_async_copy(rfr, rfr, frecv).wait()
        pltpu.make_async_copy(others, others, fsend).wait()

    @pl.when(me >= SPILL)
    def _():
        pltpu.make_async_copy(fbuf, fbuf, fsend).wait()


def layer_kernel(
    codes, slabs, rfr, vmat, slots, out, outf, wmsg, recv, acc, accf, fvm, slab_sem, sem
):
    me = lax.axis_index("patch")
    spill_copy = pltpu.make_async_copy(rfr, fvm, sem)

    @pl.when(me < SPILL)
    def _():
        spill_copy.start()

    def slab_copy(i):
        part = pl.ds(4 * i, 4)
        return pltpu.make_async_copy(slabs.at[part], recv.at[part], slab_sem.at[i])

    for i in range(4):
        slab_copy(i).start()

    for q in range(2):
        rows = [slots[:, 4 * q + b, 0:256] for b in range(4)]
        tiles = slots[:, 4 * q, 256:384][:, 1:2]
        at = slice(NP * q, NP * q + NP)
        cols = [rows[2].astype(bf16), rows[3].astype(bf16)]
        for r in range(NV):
            quarter = r % 4
            wmsg[r, at, 0:256] = cols[0]
            wmsg[r, at, 256:512] = cols[1]
            piece = rows[quarter // 2][:, 128 * (quarter % 2) : 128 * (quarter % 2) + 128]
            for side in range(2):
                mine = tiles == float(2 * (r // 4) + side)
                wmsg[r, at, 512 + 128 * side : 640 + 128 * side] = jnp.where(
                    mine, piece, 0.0
                ).astype(bf16)

    zero = jnp.zeros((ROWS, 256), f32)

    def clear(b, carry):
        for v in range(2):
            for t in range(2):
                acc[v, t, b] = zero
        return carry

    lax.fori_loop(0, 66, clear, 0, unroll=2)

    def add(at, carry):
        s = at % NS
        code = codes[at]
        tile = code % 4
        g = 2 * (code // 4) + tile % 2
        t = tile // 2
        data = recv[at // NS, s].astype(f32)
        acc[s // 4, t, 2 * g + 1] += data[:, 0:256]
        acc[s // 4, t, 2 * g + 2] += data[:, 256:512]
        return carry

    for i in range(4):
        slab_copy(i).wait()
        lax.fori_loop(4 * i * NS, 4 * (i + 1) * NS, add, 0, unroll=4)

    def smooth(blocks_of, count):
        total = None
        rows = blocks_of(0).shape[0] // (count + 2)
        for v in range(2):
            block = blocks_of(v)
            part = dot(block[rows : (count + 1) * rows], vmat[v, 128:384])
            part += dot(block[0 : count * rows, 128:256], vmat[v, 0:128])
            part += dot(block[2 * rows : (count + 2) * rows, 0:128], vmat[v, 384:512])
            total = part if total is None else total + part
        return total

    for t in range(2):
        for c in range(4):
            total = smooth(
                lambda v: acc[v, t, 16 * c : 16 * c + 18].reshape(18 * ROWS, 256).astype(bf16), 16
            )
            out[t, 16 * c : 16 * c + 16] = total.astype(bf16).reshape(16, ROWS, 256)

    @pl.when(me < SPILL)
    def _():
        accf[...] = jnp.zeros_like(accf)
        spill_copy.wait()
        target = lax.broadcasted_iota(jnp.int32, (8, S), 0) // 2

        def add_spill(c, carry):
            rows = fvm[c].astype(f32)
            for s in range(NS):
                code = codes[c * NS + s]
                tile = code % 4
                g = 2 * (code // 4) + tile % 2
                two = rows[2 * s : 2 * s + 2]
                data = jnp.where(
                    target == 1 - tile // 2, jnp.concatenate([two, two, two, two], axis=0), 0.0
                )
                accf[s // 4, 2 * g + 1] += data[:, 0:256]
                accf[s // 4, 2 * g + 2] += data[:, 256:512]
            return carry

        lax.fori_loop(0, NP, add_spill, 0)
        blocks = smooth(lambda v: accf[v].reshape(66 * 8, 256).astype(bf16), 64)
        blocks = blocks.reshape(8, 2, 32, 256)
        packed = blocks[:, 0] + pltpu.roll(blocks[:, 1], 4, 1)
        outf[...] = packed.reshape(256, 256).astype(bf16)


def owner_kernel(
    slab, spill, wmsg, moment, pick_row, pick_col, flux, weight, hess,
    part, summed, frecv, wrecv, spart, ssum, srecv,
    part_send, part_recv, sum_send, sum_recv, wsend_sem, wrecv_sem,
    spart_send, spart_recv, ssum_send, ssum_recv, mrecv, msend_sem, mrecv_sem,
):
    me_v = lax.axis_index("visit")
    me = lax.axis_index("patch")

    turn = 3 * me_v + 2 * me

    def group(v):
        return lax.rem(v + me // 2, NV)

    mine_group = group(me_v)
    barrier = pltpu.get_barrier_semaphore()

    def greet(v, p):
        pl.semaphore_signal(
            barrier, inc=1, device_id={"visit": v, "patch": p}, device_id_type=MESH
        )

    def greet_visit(j, carry):
        greet(lax.rem(me_v + j, NV), me)
        return carry

    lax.fori_loop(1, NV, greet_visit, 0)
    upper = me_v // 4

    def sender(k):
        return lax.rem(me // 2 - k // 2 + NV, NV)

    for slot in range(4):
        block = 4 * lax.rem(me_v, 4) + slot
        k = block + upper * (NP - 1 - 2 * block)
        v = sender(k)

        @pl.when(jnp.logical_not((v == me_v) & (k == me)))
        def _():
            greet(v, k)

    @pl.when((me_v == 3) | (me_v == 4))
    def _():
        def greet_spill(k, carry):
            v = sender(k)

            @pl.when(jnp.logical_not((v == me_v) & (k == me)))
            def _():
                greet(v, k)

            return carry

        lax.fori_loop(0, SPILL, greet_spill, 0)

    inside = (me // 2 == mine_group).astype(jnp.int32)
    lower_here = (me_v == me // 4).astype(jnp.int32)
    upper_here = (me_v == 4 + (NP - 1 - me) // 4).astype(jnp.int32)
    edge = ((me_v == 3) | (me_v == 4)).astype(jnp.int32)
    spills = (me < SPILL).astype(jnp.int32)
    pl.semaphore_wait(
        barrier,
        NV - 1 + 4 - inside * (lower_here + upper_here) + spills * (4 - inside * edge),
    )

    def send_moment(j, carry):
        pltpu.make_async_remote_copy(
            src_ref=moment,
            dst_ref=mrecv.at[me_v],
            send_sem=msend_sem,
            recv_sem=mrecv_sem,
            device_id={"visit": lax.rem(me_v + j, NV)},
            device_id_type=MESH,
        ).start()
        return carry


    for t in range(2):

        def send_part(j, carry):
            r = lax.rem(me_v + 1 + lax.rem(turn + j, NV - 1), NV)
            pltpu.make_async_remote_copy(
                src_ref=slab.at[t, pl.ds(8 * group(r), 8)],
                dst_ref=part.at[t, me_v],
                send_sem=part_send.at[t],
                recv_sem=part_recv.at[t],
                device_id={"visit": r},
                device_id_type=MESH,
            ).start()
            return carry

        lax.fori_loop(0, NV - 1, send_part, 0)
        pltpu.make_async_copy(
            slab.at[t, pl.ds(8 * mine_group, 8)], part.at[t, me_v], part_recv.at[t]
        ).start()

    @pl.when(me < SPILL)
    def _():
        def send_spill(j, carry):
            r = lax.rem(me_v + j, NV)
            pltpu.make_async_remote_copy(
                src_ref=spill.at[pl.ds(pl.multiple_of(32 * group(r), 32), 32)],
                dst_ref=spart.at[me_v],
                send_sem=spart_send,
                recv_sem=spart_recv,
                device_id={"visit": r},
                device_id_type=MESH,
            ).start()
            return carry

        lax.fori_loop(1, NV, send_spill, 0)
        pltpu.make_async_copy(
            spill.at[pl.ds(pl.multiple_of(32 * mine_group, 32), 32)], spart.at[me_v], spart_recv
        ).start()

    def send_weight(j, carry):
        r = lax.rem(me_v + j, NV)
        pltpu.make_async_remote_copy(
            src_ref=wmsg.at[r],
            dst_ref=wrecv.at[me_v],
            send_sem=wsend_sem,
            recv_sem=wrecv_sem,
            device_id={"visit": r},
            device_id_type=MESH,
        ).start()
        return carry

    lax.fori_loop(1, NV, send_weight, 0)
    lax.fori_loop(1, NV, send_moment, 0)
    pltpu.make_async_copy(moment, mrecv.at[me_v], mrecv_sem).start()
    pltpu.make_async_copy(wmsg.at[me_v], wrecv.at[me_v], wrecv_sem).start()

    for t in range(2):
        block = me if t == 0 else NP - 1 - me
        r = 4 * t + block // 4
        slot = lax.rem(block, 4)
        pltpu.make_async_copy(part.at[t], part.at[t], part_recv.at[t]).wait()

        def add(b, carry):
            total = part[t, 0, b].astype(f32)
            for v in range(1, NV):
                total += part[t, v, b].astype(f32)
            summed[t, b] = total.astype(bf16)
            return carry

        lax.fori_loop(0, 8, add, 0)
        for half in range(2):
            p = 2 * mine_group + half
            mine = (r == me_v) & (p == me)
            src = summed.at[t, 4 * half : 4 * half + 4]

            @pl.when(jnp.logical_not(mine))
            def _():
                pltpu.make_async_remote_copy(
                    src_ref=src,
                    dst_ref=frecv.at[slot],
                    send_sem=sum_send.at[t, half],
                    recv_sem=sum_recv,
                    device_id={"visit": r, "patch": p},
                    device_id_type=MESH,
                ).start()

            @pl.when(mine)
            def _():
                pltpu.make_async_copy(src, frecv.at[slot], sum_recv).start()

    def spill_legs(act):
        for half in range(2):
            for t in range(2):
                act(half, t, (me_v == 3 + t) & (me == 2 * mine_group + half))

    @pl.when(me < SPILL)
    def _():
        pltpu.make_async_copy(spart, spart, spart_recv).wait()
        total = spart[0].astype(f32)
        for v in range(1, NV):
            total += spart[v].astype(f32)
        ssum[...] = total.astype(bf16)

        def leg(half, t, mine):
            src = ssum

            @pl.when(jnp.logical_not(mine))
            def _():
                pltpu.make_async_remote_copy(
                    src_ref=src,
                    dst_ref=srecv.at[me],
                    send_sem=ssum_send.at[t, half],
                    recv_sem=ssum_recv,
                    device_id={"visit": 3 + t, "patch": 2 * mine_group + half},
                    device_id_type=MESH,
                ).start()

            @pl.when(mine)
            def _():
                pltpu.make_async_copy(src, srecv.at[me], ssum_recv).start()

        spill_legs(leg)

    pltpu.make_async_copy(wrecv, wrecv, wrecv_sem).wait()
    cols = wrecv[:, :, 0:512].reshape(NV * 2 * NP, 512)
    left = wrecv[:, :, 512:640].reshape(NV * 2 * NP, 128)
    right = wrecv[:, :, 640:768].reshape(NV * 2 * NP, 128)
    weight[:, 0:512] = dot_tn(left, cols)
    weight[:, 512:1024] = dot_tn(right, cols)
    pltpu.make_async_copy(mrecv, mrecv, mrecv_sem).wait()
    total = mrecv[0]
    for v in range(1, NV):
        total += mrecv[v]
    picked = dot(pick_row[...], total, precise) * pick_col[...]
    sums = jnp.sum(picked, axis=1, keepdims=True)
    lane = lax.broadcasted_iota(jnp.int32, (16, 128), 1)
    matrix = jnp.zeros((16, 128), f32)
    for q in range(10):
        matrix = jnp.where(lane == q, sums[16 * q : 16 * q + 16], matrix)
    hess[0] = matrix[0:10, 0:10] * (1.0 / (NV * 2 * 4 * S * S))
    pltpu.make_async_copy(mrecv.at[1:NV], mrecv.at[1:NV], msend_sem).wait()
    pltpu.make_async_copy(frecv, frecv, sum_recv).wait()
    for slot in range(4):
        for q in range(4):
            flux[32 * slot : 32 * slot + 32, 256 * q : 256 * q + 256] = frecv[slot, q].astype(f32)
    for t in range(2):

        @pl.when(me_v == 3 + t)
        def _():
            pltpu.make_async_copy(srecv, srecv, ssum_recv).wait()
            odd = lax.rem(me, 2) == 1
            for k in range(SPILL):
                got = srecv[k].astype(f32)
                rows8 = [
                    jnp.where(odd, got[8 * q + 4 : 8 * q + 8], got[8 * q : 8 * q + 4])
                    for q in range(4)
                ]
                for e in range(2):
                    at = 2 * k + e
                    line = at if t == 1 else 127 - at
                    for q in range(4):
                        flux[line : line + 1, 256 * q : 256 * q + 256] += rows8[q][
                            2 * t + e : 2 * t + e + 1
                        ]

    @pl.when(me < SPILL)
    def _():
        pltpu.make_async_copy(spart.at[1:NV], spart.at[1:NV], spart_send).wait()

        def leg_sent(half, t, mine):
            @pl.when(jnp.logical_not(mine))
            def _():
                src = ssum
                pltpu.make_async_copy(src, src, ssum_send.at[t, half]).wait()

        spill_legs(leg_sent)

    pltpu.make_async_copy(wrecv.at[1:NV], wrecv.at[1:NV], wsend_sem).wait()
    for t in range(2):
        block = me if t == 0 else NP - 1 - me
        r = 4 * t + block // 4
        pltpu.make_async_copy(part.at[t, 1:NV], part.at[t, 1:NV], part_send.at[t]).wait()
        for half in range(2):
            mine = (r == me_v) & (2 * mine_group + half == me)

            @pl.when(jnp.logical_not(mine))
            def _():
                src = summed.at[t, 4 * half : 4 * half + 4]
                pltpu.make_async_copy(src, src, sum_send.at[t, half]).wait()


def body(
    pixels, row_mask, col_mask, route, tile, wcs_offset, subpixel, plate_scale, stretch_weight, psf_taps
):
    pix = pixels.reshape(NS, S, S)
    params = jnp.concatenate(
        [
            plate_scale[..., None].astype(f32),
            wcs_offset.astype(f32),
            subpixel.astype(f32),
            stretch_weight[..., None].astype(f32),
        ],
        axis=-1,
    )
    outer = outer_tables()
    outer_x = np.pad(outer.astype(np.float32), ((0, 0), (0, 112), (0, 0)))
    vm = pl.BlockSpec(memory_space=pltpu.VMEM)
    sm = pl.BlockSpec(memory_space=pltpu.SMEM)
    hbm = pl.BlockSpec(memory_space=pl.ANY)
    dma = pltpu.SemaphoreType.DMA
    recv, rfr, rsmall, moments, vmat = pl.pallas_call(
        warp_kernel,
        out_shape=(
            jax.ShapeDtypeStruct((NP, NS, ROWS, S), bf16),
            jax.ShapeDtypeStruct((NP, 16, S), bf16),
            jax.ShapeDtypeStruct((NP, 8, 384), f32),
            jax.ShapeDtypeStruct((16, 128), f32),
            jax.ShapeDtypeStruct((2, 512, 256), bf16),
        ),
        in_specs=[sm, sm, sm, hbm, vm, vm, vm, vm, vm],
        out_specs=(hbm, hbm, hbm, vm, vm),
        scratch_shapes=[
            pltpu.VMEM((NS, S, S), bf16),
            pltpu.VMEM((8, 256), f32),
            pltpu.VMEM((NS, S, S), bf16),
            pltpu.VMEM((16 * SPILL, S), bf16),
            pltpu.VMEM((896, S), bf16),
            pltpu.VMEM((S, S), bf16),
            pltpu.VMEM((S, S), bf16),
            pltpu.VMEM((NS, 128, S), bf16),
            pltpu.VMEM((2, 128, 256), bf16),
            pltpu.VMEM((8, 2 * S), f32),
            pltpu.VMEM((2, 16, S), f32),
            pltpu.VMEM((128, 384), f32),
            dma((NS,)), dma((NS,)), dma((NS,)),
            dma, dma, dma, dma,
        ],
        compiler_params=pltpu.CompilerParams(
            has_side_effects=True, vmem_limit_bytes=60 * 1024 * 1024, collective_id=1
        ),
        name="warp_send",
    )(params, route, tile, pix, row_mask, col_mask, psf_taps, outer, outer_x)

    codes = rsmall[:, :, 256].reshape(NP * NS).astype(jnp.int32)
    slab, spill, wmsg = pl.pallas_call(
        layer_kernel,
        out_shape=(
            jax.ShapeDtypeStruct((2, 64, ROWS, 256), bf16),
            jax.ShapeDtypeStruct((256, 256), bf16),
            jax.ShapeDtypeStruct((NV, 2 * NP, 768), bf16),
        ),
        in_specs=[sm, hbm, hbm, vm, vm],
        out_specs=(vm, vm, vm),
        scratch_shapes=[
            pltpu.VMEM((NP, NS, ROWS, S), bf16),
            pltpu.VMEM((2, 2, 66, ROWS, 256), f32),
            pltpu.VMEM((2, 66, 8, 256), f32),
            pltpu.VMEM((NP, 16, S), bf16),
            dma((4,)),
            dma,
        ],
        compiler_params=pltpu.CompilerParams(vmem_limit_bytes=60 * 1024 * 1024),
        name="layer_smooth",
    )(codes, recv, rfr, vmat, rsmall)

    pick_row = np.zeros((160, 16), np.float32)
    pick_col = np.zeros((160, 128), np.float32)
    for q in range(10):
        for r in range(10):
            pick_row[16 * q + r, 4 * PAIRS[q][0] + PAIRS[r][0]] = 1
            pick_col[16 * q + r, 4 * PAIRS[q][1] + PAIRS[r][1]] = 1
    flux, weight, hessian = pl.pallas_call(
        owner_kernel,
        out_shape=(
            jax.ShapeDtypeStruct((128, 2 * S), f32),
            jax.ShapeDtypeStruct((128, 2 * S), f32),
            jax.ShapeDtypeStruct((1, 10, 10), f32),
        ),
        in_specs=[hbm, hbm, hbm, hbm, vm, vm],
        out_specs=(vm, vm, vm),
        scratch_shapes=[
            pltpu.VMEM((2, NV, 8, ROWS, 256), bf16),
            pltpu.VMEM((2, 8, ROWS, 256), bf16),
            pltpu.VMEM((4, 4, ROWS, 256), bf16),
            pltpu.VMEM((NV, 2 * NP, 768), bf16),
            pltpu.VMEM((NV, 32, 256), bf16),
            pltpu.VMEM((32, 256), bf16),
            pltpu.VMEM((SPILL, 32, 256), bf16),
            dma((2,)), dma((2,)), dma((2, 2)), dma, dma, dma,
            dma, dma, dma((2, 2)), dma,
            pltpu.VMEM((NV, 16, 128), f32),
            dma, dma,
        ],
        compiler_params=pltpu.CompilerParams(
            has_side_effects=True, vmem_limit_bytes=48 * 1024 * 1024, collective_id=2
        ),
        name="owner_sum",
    )(slab, spill, wmsg, moments, pick_row, pick_col)

    return flux, weight, hessian


def solution(mesh):
    in_specs = (
        P("patch", "visit", None, None, None),
        P("patch", "visit", None, None),
        P("patch", "visit", None, None),
        P("patch", "visit", None),
        P("patch", "visit", None),
        P("patch", "visit", None, None),
        P("patch", "visit", None, None),
        P("patch", "visit", None),
        P("patch", "visit", None),
        P("visit", None, None),
    )
    out_specs = (P("visit", "patch"), P("visit", "patch"), P("patch", None, None))
    return jax.shard_map(body, mesh=mesh, in_specs=in_specs, out_specs=out_specs, check_vma=False)
```

```python
import jax
import jax.numpy as jnp
import numpy as np
from jax import lax
from jax.experimental import pallas as pl
from jax.experimental.pallas import tpu as pltpu
from jax.sharding import PartitionSpec as P

PAIRS = ((0, 0), (1, 0), (0, 1), (2, 0), (1, 1), (0, 2), (3, 0), (2, 1), (1, 2), (0, 3))
MESH = pl.DeviceIdType.MESH
precise = lax.Precision.HIGHEST
f32 = jnp.float32
bf16 = jnp.bfloat16
S = 512
TAPS = 41
NP = 16
NV = 8
NS = 8
ROWS = S // NP
SPILL = 10


def lanczos(offset):
    wide = offset * np.float32(np.pi)
    narrow = wide * np.float32(1.0 / 3.0)
    product = wide * narrow
    ratio = jnp.sin(wide) * jnp.sin(narrow) / jnp.where(product == 0.0, 1.0, product)
    value = jnp.where(product == 0.0, 1.0, ratio)
    return jnp.where(jnp.abs(offset) < 3.0, value, 0.0)


def outer_tables():
    grid_pos = np.arange(S, dtype=np.float32)
    block = np.arange(2, dtype=np.float32)
    coord = (block[:, None] * np.float32(S) + grid_pos[None, :] + np.float32(0.5)) / np.float32(
        S
    ) - np.float32(1.0)
    square = coord * coord
    poly = np.stack(
        [
            np.ones_like(coord),
            coord,
            np.float32(1.5) * square - np.float32(0.5),
            (np.float32(2.5) * square - np.float32(1.5)) * coord,
        ],
        axis=1,
    )
    return (poly[:, :, None, :] * poly[:, None, :, :]).reshape(2, 16, S).astype(bf16)


def dot(a, b, precision=None):
    return jnp.dot(a, b, preferred_element_type=f32, precision=precision)


def dot_nt(a, b, precision=None):
    return lax.dot_general(
        a, b, (((1,), (1,)), ((), ())), preferred_element_type=f32, precision=precision
    )


def dot_tn(a, b):
    return lax.dot_general(a, b, (((0,), (0,)), ((), ())), preferred_element_type=f32)


def band(position, base, weight_of):
    offset = position - base
    value = jnp.zeros(offset.shape, f32)
    for k in range(6):
        value = jnp.where(offset == float(k), weight_of(k), value)
    return value


def spill_row(row):
    return 2 * (row // 16) + row % 2


def sheared(line, rows):
    return pltpu.roll(
        jnp.broadcast_to(line, (rows, line.shape[1])), 0, 1, stride=1, stride_axis=0
    )


def warp_kernel(
    params, route, tile, pixels, row_masks, col_masks, psf, oy, ox,
    recv, rfr, rsmall, hess, vmat,
    pix, lines, sbuf, fbuf, wpad, ybuf, half, edges, umat, cov, rmom, small,
    pix_sem, send_sem, recv_sem, fsend, frecv, ssend, srecv,
):
    me_v = lax.axis_index("visit")
    me = lax.axis_index("patch")
    barrier = pltpu.get_barrier_semaphore()

    def greet(j, carry):
        pl.semaphore_signal(
            barrier, inc=1, device_id={"patch": lax.rem(me + j, NP)}, device_id_type=MESH
        )
        return carry

    lax.fori_loop(1, NP, greet, 0)

    def pixel_copy(s):
        return pltpu.make_async_copy(pixels.at[s], pix.at[s], pix_sem.at[s])

    for s in range(NS):
        pixel_copy(s).start()
    lines[...] = jnp.zeros_like(lines)
    wpad[0:192, :] = jnp.zeros((192, S), bf16)
    wpad[704:896, :] = jnp.zeros((192, S), bf16)
    rmom[...] = jnp.zeros_like(rmom)
    tap_lines = []
    for v in range(2):
        kernels = psf[v] / jnp.sum(psf[v], axis=1, keepdims=True)
        lines[2 * v : 2 * v + 2, 0:TAPS] = kernels.astype(bf16).astype(f32)
        placed = pltpu.roll(lines[...], 44, 1)
        tap_lines.append(placed[2 * v : 2 * v + 2])
        umat[v] = sheared(placed[2 * v + 1 : 2 * v + 2], 128).astype(bf16)

    def stretch(s):
        v = s // 4
        piece = s % 4
        is_low = tile[0, v, piece] < 2
        spot = lax.broadcasted_iota(jnp.int32, (8, S), 1).astype(f32) - 256.0
        tap = lax.broadcasted_iota(jnp.int32, (8, S), 0).astype(f32)

        def weights_along(axis, factor):
            shift = params[0, v, piece, 1 + axis] + params[0, v, piece, 3 + axis]
            source = params[0, v, piece, 0] * spot + (256.0 + shift)
            lowest = jnp.floor(source) - 2.0
            value = (factor * lanczos((lowest + tap) - source)).astype(bf16).astype(f32)
            return jnp.where(tap == 6.0, lowest, value)

        columns = jnp.transpose(weights_along(0, 1.0))
        pixel_copy(s).wait()
        wt = weights_along(1, params[0, v, piece, 5])
        row_mask = row_masks[0, v, pl.ds(piece, 1), :].astype(f32)
        col_mask = col_masks[0, v, pl.ds(piece, 1), :].astype(f32)
        ones = jnp.ones((8, 384), bf16)
        for a in range(2):
            at = lax.broadcasted_iota(jnp.int32, (256, 384), 1).astype(f32) + float(128 * a)
            cols = columns[256 * a : 256 * a + 256]
            weights = band(at, cols[:, 6:7], lambda k: cols[:, k : k + 1])
            rows_map = (weights * row_mask[:, 128 * a : 128 * a + 384]).astype(bf16)
            part = dot(rows_map, pix[s, 128 * a : 128 * a + 384, :])
            half[256 * a : 256 * a + 256, :] = (part * col_mask).astype(bf16)
            cover = dot_nt(ones, rows_map)
            cov[pl.ds(s, 1), 256 * a : 256 * a + 256] = cover[0:1]
        for b in range(2):
            at = lax.broadcasted_iota(jnp.int32, (384, 256), 0).astype(f32) + float(128 * b)
            lanes = wt[:, 256 * b : 256 * b + 256]
            cols_map = band(at, lanes[6:7], lambda k: lanes[k : k + 1]).astype(bf16)
            part = dot(half[:, 128 * b : 128 * b + 384], cols_map)
            wpad[192:704, 256 * b : 256 * b + 256] = part.astype(bf16)
            mask = jnp.broadcast_to(col_mask[:, 128 * b : 128 * b + 384], (8, 384)).astype(bf16)
            cover = dot(mask, cols_map)
            cov[pl.ds(s, 1), S + 256 * b : S + 256 * b + 256] = cover[0:1]
        for a in range(4):
            ybuf[128 * a : 128 * a + 128, :] = dot(
                umat[v], wpad[128 + 128 * a : 384 + 128 * a, :]
            ).astype(bf16)
        for q in range(NP):
            low = ybuf[ROWS * q : ROWS * (q + 1), :]
            high = ybuf[ROWS * (NP - 1 - q) : ROWS * (NP - q), :]
            sbuf[s, ROWS * q : ROWS * (q + 1), :] = jnp.where(is_low, low, high)
        edges[s, 0:64] = wpad[192:256, :]
        edges[s, 64:128] = wpad[640:704, :]

    turn = 7 * me + 3 * me_v

    def send_slabs(s):
        def send(j, carry):
            k = lax.rem(me + 1 + lax.rem(turn + j, NP - 1), NP)
            pltpu.make_async_remote_copy(
                src_ref=sbuf.at[s, pl.ds(pl.multiple_of(k * ROWS, ROWS), ROWS)],
                dst_ref=recv.at[me, s],
                send_sem=send_sem.at[s],
                recv_sem=recv_sem.at[s],
                device_id={"patch": k},
                device_id_type=MESH,
            ).start()
            return carry

        lax.fori_loop(0, NP - 1, send, 0)
        pltpu.make_async_copy(
            sbuf.at[s, pl.ds(pl.multiple_of(me * ROWS, ROWS), ROWS)], recv.at[me, s], recv_sem.at[s]
        ).start()

    stretch(0)
    pl.semaphore_wait(barrier, NP - 1)

    def step(s, carry):
        send_slabs(s)
        stretch(s + 1)
        return carry

    lax.fori_loop(0, NS - 1, step, 0)
    send_slabs(NS - 1)

    row = lax.broadcasted_iota(jnp.int32, (16 * SPILL, 128), 0)
    lane = lax.broadcasted_iota(jnp.int32, (16 * SPILL, 128), 1)
    spilled = jnp.zeros((16 * SPILL, S), f32)
    step_row = spill_row(lax.broadcasted_iota(jnp.int32, (16 * SPILL, 32), 0))
    step_lane = lax.broadcasted_iota(jnp.int32, (16 * SPILL, 32), 1)
    forward = jnp.where(step_lane == step_row, 1.0, 0.0).astype(bf16)
    backward = jnp.where(step_lane == 31 - step_row, 1.0, 0.0).astype(bf16)
    for v in range(2):
        wide = jnp.concatenate([tap_lines[v][1:2], jnp.zeros((1, 256), f32)], axis=1)
        below = sheared(pltpu.roll(wide, 64, 1), 32)[:, 0:128].astype(bf16)
        above = sheared(pltpu.roll(wide, 416, 1), 32)[:, 0:128].astype(bf16)
        taps = jnp.where(lane >= 64, dot(forward, below), dot(backward, above))
        for s in range(4 * v, 4 * v + 4):
            keep = (row % 16 // 2 == s) & (lane // 64 == 1 - tile[0, v, s - 4 * v] // 2)
            spilled += dot(jnp.where(keep, taps, 0.0).astype(bf16), edges[s])
    fbuf[...] = spilled.astype(bf16)

    def send_spill(k, carry):
        src = fbuf.at[pl.ds(pl.multiple_of(16 * k, 16), 16)]

        @pl.when(me != k)
        def _():
            pltpu.make_async_remote_copy(
                src_ref=src,
                dst_ref=rfr.at[me],
                send_sem=fsend,
                recv_sem=frecv,
                device_id={"patch": k},
                device_id_type=MESH,
            ).start()

        @pl.when(me == k)
        def _():
            pltpu.make_async_copy(src, rfr.at[me], frecv).start()

        return carry

    lax.fori_loop(0, SPILL, send_spill, 0)

    def moments(s, carry):
        piece = s % 4
        values = pix[s].astype(f32)
        square = (values * values).astype(bf16)
        v = s // 4
        lhs = oy[piece // 2] * row_masks[0, v, pl.ds(piece, 1), :].astype(f32).astype(bf16)
        col_mask = col_masks[0, v, pl.ds(piece, 1), :].astype(f32)
        rmom[piece % 2] += dot(lhs, square) * (col_mask * params[0, v, piece, 5])
        return carry

    lax.fori_loop(0, NS, moments, 0)
    row = lax.broadcasted_iota(jnp.int32, (8 * NP, 256), 0)
    slots = jnp.zeros((8 * NP, 256), f32)
    line = lax.broadcasted_iota(jnp.int32, (8 * NP, 128), 0)
    codes = jnp.zeros((8 * NP, 128), f32)
    slot_tile = jnp.zeros((8 * NP, 128), f32)
    routes = [route[0, s // 4, s % 4] for s in range(NS)]
    for s in range(NS):
        rank = jnp.int32(0)
        for before in range(s):
            rank += (routes[before] == routes[s]).astype(jnp.int32)
        cover = cov[s : s + 1].astype(bf16).astype(f32)
        values = cover[:, 0:256]
        for b in range(1, 4):
            values = jnp.where(row % 4 == b, cover[:, 256 * b : 256 * b + 256], values)
        slots += jnp.where((row // 8 == routes[s]) & (row % 8 // 4 == rank), values, 0.0)
        mine = tile[0, s // 4, s % 4]
        codes = jnp.where(line % 8 == s, (4 * routes[s] + mine).astype(f32), codes)
        slot_tile = jnp.where(
            (line // 8 == routes[s]) & (line % 8 // 4 == rank), mine.astype(f32), slot_tile
        )
    small[:, 0:256] = slots
    lane = lax.broadcasted_iota(jnp.int32, (8 * NP, 128), 1)
    small[:, 256:384] = jnp.where(lane == 0, codes, slot_tile)
    hess[...] = dot_nt(rmom[0], ox[0], precise) + dot_nt(rmom[1], ox[1], precise)

    def send_small(j, carry):
        k = lax.rem(me + j, NP)
        pltpu.make_async_remote_copy(
            src_ref=small.at[pl.ds(pl.multiple_of(k * 8, 8), 8)],
            dst_ref=rsmall.at[me],
            send_sem=ssend,
            recv_sem=srecv,
            device_id={"patch": k},
            device_id_type=MESH,
        ).start()
        return carry

    lax.fori_loop(1, NP, send_small, 0)
    pltpu.make_async_copy(
        small.at[pl.ds(pl.multiple_of(me * 8, 8), 8)], rsmall.at[me], srecv
    ).start()

    for v in range(2):
        wide = jnp.concatenate([tap_lines[v][0:1], jnp.zeros((1, 256), f32)], axis=1)
        for c in range(2):
            part = sheared(pltpu.roll(wide, 64 + 128 * c, 1), 128)
            vmat[v, :, 128 * c : 128 * c + 128] = jnp.transpose(part).astype(bf16)

    pltpu.make_async_copy(rsmall, rsmall, srecv).wait()
    pltpu.make_async_copy(rsmall.at[1:NP], rsmall.at[1:NP], ssend).wait()

    def finish(i, carry):
        everyone = recv.at[:, i]
        others = recv.at[1:NP, i]
        pltpu.make_async_copy(everyone, everyone, recv_sem.at[i]).wait()
        pltpu.make_async_copy(others, others, send_sem.at[i]).wait()
        return carry

    lax.fori_loop(0, NS, finish, 0)

    @pl.when(me < SPILL)
    def _():
        others = fbuf.at[0 : 16 * (SPILL - 1)]
        pltpu.make_async_copy(rfr, rfr, frecv).wait()
        pltpu.make_async_copy(others, others, fsend).wait()

    @pl.when(me >= SPILL)
    def _():
        pltpu.make_async_copy(fbuf, fbuf, fsend).wait()


def layer_kernel(
    codes, slabs, rfr, vmat, slots, out, outf, wmsg, recv, acc, accf, fvm, slab_sem, sem
):
    me = lax.axis_index("patch")
    spill_copy = pltpu.make_async_copy(rfr, fvm, sem)

    @pl.when(me < SPILL)
    def _():
        spill_copy.start()

    def slab_copy(i):
        part = pl.ds(4 * i, 4)
        return pltpu.make_async_copy(slabs.at[part], recv.at[part], slab_sem.at[i])

    for i in range(4):
        slab_copy(i).start()

    for q in range(2):
        rows = [slots[:, 4 * q + b, 0:256] for b in range(4)]
        tiles = slots[:, 4 * q, 256:384][:, 1:2]
        at = slice(NP * q, NP * q + NP)
        cols = [rows[2].astype(bf16), rows[3].astype(bf16)]
        for r in range(NV):
            quarter = r % 4
            wmsg[r, at, 0:256] = cols[0]
            wmsg[r, at, 256:512] = cols[1]
            piece = rows[quarter // 2][:, 128 * (quarter % 2) : 128 * (quarter % 2) + 128]
            for side in range(2):
                mine = tiles == float(2 * (r // 4) + side)
                wmsg[r, at, 512 + 128 * side : 640 + 128 * side] = jnp.where(
                    mine, piece, 0.0
                ).astype(bf16)

    zero = jnp.zeros((ROWS, 256), f32)

    def clear(b, carry):
        for v in range(2):
            for t in range(2):
                acc[v, t, b] = zero
        return carry

    lax.fori_loop(0, 66, clear, 0, unroll=2)

    def add(at, carry):
        s = at % NS
        code = codes[at]
        tile = code % 4
        g = 2 * (code // 4) + tile % 2
        t = tile // 2
        data = recv[at // NS, s].astype(f32)
        acc[s // 4, t, 2 * g + 1] += data[:, 0:256]
        acc[s // 4, t, 2 * g + 2] += data[:, 256:512]
        return carry

    for i in range(4):
        slab_copy(i).wait()
        lax.fori_loop(4 * i * NS, 4 * (i + 1) * NS, add, 0, unroll=4)

    def smooth(blocks_of, count):
        total = None
        rows = blocks_of(0).shape[0] // (count + 2)
        for v in range(2):
            block = blocks_of(v)
            part = dot(block[rows : (count + 1) * rows], vmat[v, 128:384])
            part += dot(block[0 : count * rows, 128:256], vmat[v, 0:128])
            part += dot(block[2 * rows : (count + 2) * rows, 0:128], vmat[v, 384:512])
            total = part if total is None else total + part
        return total

    for t in range(2):
        for c in range(4):
            total = smooth(
                lambda v: acc[v, t, 16 * c : 16 * c + 18].reshape(18 * ROWS, 256).astype(bf16), 16
            )
            out[t, 16 * c : 16 * c + 16] = total.astype(bf16).reshape(16, ROWS, 256)

    @pl.when(me < SPILL)
    def _():
        accf[...] = jnp.zeros_like(accf)
        spill_copy.wait()
        target = lax.broadcasted_iota(jnp.int32, (8, S), 0) // 2

        def add_spill(c, carry):
            rows = fvm[c].astype(f32)
            for s in range(NS):
                code = codes[c * NS + s]
                tile = code % 4
                g = 2 * (code // 4) + tile % 2
                two = rows[2 * s : 2 * s + 2]
                data = jnp.where(
                    target == 1 - tile // 2, jnp.concatenate([two, two, two, two], axis=0), 0.0
                )
                accf[s // 4, 2 * g + 1] += data[:, 0:256]
                accf[s // 4, 2 * g + 2] += data[:, 256:512]
            return carry

        lax.fori_loop(0, NP, add_spill, 0)
        blocks = smooth(lambda v: accf[v].reshape(66 * 8, 256).astype(bf16), 64)
        blocks = blocks.reshape(8, 2, 32, 256)
        packed = blocks[:, 0] + pltpu.roll(blocks[:, 1], 4, 1)
        outf[...] = packed.reshape(256, 256).astype(bf16)


def owner_kernel(
    slab, spill, wmsg, moment, pick_row, pick_col, flux, weight, hess,
    part, summed, frecv, wrecv, spart, ssum, srecv,
    part_send, part_recv, sum_send, sum_recv, wsend_sem, wrecv_sem,
    spart_send, spart_recv, ssum_send, ssum_recv, mrecv, msend_sem, mrecv_sem,
):
    me_v = lax.axis_index("visit")
    me = lax.axis_index("patch")

    turn = 3 * me_v + 2 * me

    def group(v):
        return lax.rem(v + me // 2, NV)

    mine_group = group(me_v)
    barrier = pltpu.get_barrier_semaphore()

    def greet(v, p):
        pl.semaphore_signal(
            barrier, inc=1, device_id={"visit": v, "patch": p}, device_id_type=MESH
        )

    def greet_visit(j, carry):
        greet(lax.rem(me_v + j, NV), me)
        return carry

    lax.fori_loop(1, NV, greet_visit, 0)
    upper = me_v // 4

    def sender(k):
        return lax.rem(me // 2 - k // 2 + NV, NV)

    for slot in range(4):
        block = 4 * lax.rem(me_v, 4) + slot
        k = block + upper * (NP - 1 - 2 * block)
        v = sender(k)

        @pl.when(jnp.logical_not((v == me_v) & (k == me)))
        def _():
            greet(v, k)

    @pl.when((me_v == 3) | (me_v == 4))
    def _():
        def greet_spill(k, carry):
            v = sender(k)

            @pl.when(jnp.logical_not((v == me_v) & (k == me)))
            def _():
                greet(v, k)

            return carry

        lax.fori_loop(0, SPILL, greet_spill, 0)

    inside = (me // 2 == mine_group).astype(jnp.int32)
    lower_here = (me_v == me // 4).astype(jnp.int32)
    upper_here = (me_v == 4 + (NP - 1 - me) // 4).astype(jnp.int32)
    edge = ((me_v == 3) | (me_v == 4)).astype(jnp.int32)
    spills = (me < SPILL).astype(jnp.int32)
    pl.semaphore_wait(
        barrier,
        NV - 1 + 4 - inside * (lower_here + upper_here) + spills * (4 - inside * edge),
    )

    def send_moment(j, carry):
        pltpu.make_async_remote_copy(
            src_ref=moment,
            dst_ref=mrecv.at[me_v],
            send_sem=msend_sem,
            recv_sem=mrecv_sem,
            device_id={"visit": lax.rem(me_v + j, NV)},
            device_id_type=MESH,
        ).start()
        return carry


    @pl.when(me < SPILL)
    def _():
        def send_spill(j, carry):
            r = lax.rem(me_v + j, NV)
            pltpu.make_async_remote_copy(
                src_ref=spill.at[pl.ds(pl.multiple_of(32 * group(r), 32), 32)],
                dst_ref=spart.at[me_v],
                send_sem=spart_send,
                recv_sem=spart_recv,
                device_id={"visit": r},
                device_id_type=MESH,
            ).start()
            return carry

        lax.fori_loop(1, NV, send_spill, 0)
        pltpu.make_async_copy(
            spill.at[pl.ds(pl.multiple_of(32 * mine_group, 32), 32)], spart.at[me_v], spart_recv
        ).start()

    for t in range(2):
        for half in range(2):

            def send_part(j, carry):
                r = lax.rem(me_v + 1 + lax.rem(turn + j, NV - 1), NV)
                pltpu.make_async_remote_copy(
                    src_ref=slab.at[t, pl.ds(8 * group(r) + 4 * half, 4)],
                    dst_ref=part.at[t, half, me_v],
                    send_sem=part_send.at[t, half],
                    recv_sem=part_recv.at[t, half],
                    device_id={"visit": r},
                    device_id_type=MESH,
                ).start()
                return carry

            lax.fori_loop(0, NV - 1, send_part, 0)
            pltpu.make_async_copy(
                slab.at[t, pl.ds(8 * mine_group + 4 * half, 4)],
                part.at[t, half, me_v],
                part_recv.at[t, half],
            ).start()

    def send_weight(j, carry):
        r = lax.rem(me_v + j, NV)
        pltpu.make_async_remote_copy(
            src_ref=wmsg.at[r],
            dst_ref=wrecv.at[me_v],
            send_sem=wsend_sem,
            recv_sem=wrecv_sem,
            device_id={"visit": r},
            device_id_type=MESH,
        ).start()
        return carry

    lax.fori_loop(1, NV, send_weight, 0)
    lax.fori_loop(1, NV, send_moment, 0)
    pltpu.make_async_copy(moment, mrecv.at[me_v], mrecv_sem).start()
    pltpu.make_async_copy(wmsg.at[me_v], wrecv.at[me_v], wrecv_sem).start()

    def spill_legs(act):
        for half in range(2):
            for t in range(2):
                act(half, t, (me_v == 3 + t) & (me == 2 * mine_group + half))

    @pl.when(me < SPILL)
    def _():
        pltpu.make_async_copy(spart, spart, spart_recv).wait()
        total = spart[0].astype(f32)
        for v in range(1, NV):
            total += spart[v].astype(f32)
        ssum[...] = total.astype(bf16)

        def leg(half, t, mine):
            src = ssum

            @pl.when(jnp.logical_not(mine))
            def _():
                pltpu.make_async_remote_copy(
                    src_ref=src,
                    dst_ref=srecv.at[me],
                    send_sem=ssum_send.at[t, half],
                    recv_sem=ssum_recv,
                    device_id={"visit": 3 + t, "patch": 2 * mine_group + half},
                    device_id_type=MESH,
                ).start()

            @pl.when(mine)
            def _():
                pltpu.make_async_copy(src, srecv.at[me], ssum_recv).start()

        spill_legs(leg)

    for t in range(2):
        block = me if t == 0 else NP - 1 - me
        r = 4 * t + block // 4
        slot = lax.rem(block, 4)
        for half in range(2):
            pltpu.make_async_copy(
                part.at[t, half], part.at[t, half], part_recv.at[t, half]
            ).wait()

            def add(b, carry):
                total = part[t, half, 0, b].astype(f32)
                for v in range(1, NV):
                    total += part[t, half, v, b].astype(f32)
                summed[t, 4 * half + b] = total.astype(bf16)
                return carry

            lax.fori_loop(0, 4, add, 0)
            p = 2 * mine_group + half
            mine = (r == me_v) & (p == me)
            src = summed.at[t, 4 * half : 4 * half + 4]

            @pl.when(jnp.logical_not(mine))
            def _():
                pltpu.make_async_remote_copy(
                    src_ref=src,
                    dst_ref=frecv.at[slot],
                    send_sem=sum_send.at[t, half],
                    recv_sem=sum_recv,
                    device_id={"visit": r, "patch": p},
                    device_id_type=MESH,
                ).start()

            @pl.when(mine)
            def _():
                pltpu.make_async_copy(src, frecv.at[slot], sum_recv).start()

    pltpu.make_async_copy(wrecv, wrecv, wrecv_sem).wait()
    cols = wrecv[:, :, 0:512].reshape(NV * 2 * NP, 512)
    left = wrecv[:, :, 512:640].reshape(NV * 2 * NP, 128)
    right = wrecv[:, :, 640:768].reshape(NV * 2 * NP, 128)
    weight[:, 0:512] = dot_tn(left, cols)
    weight[:, 512:1024] = dot_tn(right, cols)
    pltpu.make_async_copy(mrecv, mrecv, mrecv_sem).wait()
    total = mrecv[0]
    for v in range(1, NV):
        total += mrecv[v]
    picked = dot(pick_row[...], total, precise) * pick_col[...]
    sums = jnp.sum(picked, axis=1, keepdims=True)
    lane = lax.broadcasted_iota(jnp.int32, (16, 128), 1)
    matrix = jnp.zeros((16, 128), f32)
    for q in range(10):
        matrix = jnp.where(lane == q, sums[16 * q : 16 * q + 16], matrix)
    hess[0] = matrix[0:10, 0:10] * (1.0 / (NV * 2 * 4 * S * S))
    pltpu.make_async_copy(mrecv.at[1:NV], mrecv.at[1:NV], msend_sem).wait()
    pltpu.make_async_copy(frecv, frecv, sum_recv).wait()
    for slot in range(4):
        for q in range(4):
            flux[32 * slot : 32 * slot + 32, 256 * q : 256 * q + 256] = frecv[slot, q].astype(f32)
    for t in range(2):

        @pl.when(me_v == 3 + t)
        def _():
            pltpu.make_async_copy(srecv, srecv, ssum_recv).wait()
            odd = lax.rem(me, 2) == 1
            for k in range(SPILL):
                got = srecv[k].astype(f32)
                rows8 = [
                    jnp.where(odd, got[8 * q + 4 : 8 * q + 8], got[8 * q : 8 * q + 4])
                    for q in range(4)
                ]
                for e in range(2):
                    at = 2 * k + e
                    line = at if t == 1 else 127 - at
                    for q in range(4):
                        flux[line : line + 1, 256 * q : 256 * q + 256] += rows8[q][
                            2 * t + e : 2 * t + e + 1
                        ]

    @pl.when(me < SPILL)
    def _():
        pltpu.make_async_copy(spart.at[1:NV], spart.at[1:NV], spart_send).wait()

        def leg_sent(half, t, mine):
            @pl.when(jnp.logical_not(mine))
            def _():
                src = ssum
                pltpu.make_async_copy(src, src, ssum_send.at[t, half]).wait()

        spill_legs(leg_sent)

    pltpu.make_async_copy(wrecv.at[1:NV], wrecv.at[1:NV], wsend_sem).wait()
    for t in range(2):
        block = me if t == 0 else NP - 1 - me
        r = 4 * t + block // 4
        for half in range(2):
            others = part.at[t, half, 1:NV]
            pltpu.make_async_copy(others, others, part_send.at[t, half]).wait()
            mine = (r == me_v) & (2 * mine_group + half == me)

            @pl.when(jnp.logical_not(mine))
            def _():
                src = summed.at[t, 4 * half : 4 * half + 4]
                pltpu.make_async_copy(src, src, sum_send.at[t, half]).wait()


def body(
    pixels, row_mask, col_mask, route, tile, wcs_offset, subpixel, plate_scale, stretch_weight, psf_taps
):
    pix = pixels.reshape(NS, S, S)
    params = jnp.concatenate(
        [
            plate_scale[..., None].astype(f32),
            wcs_offset.astype(f32),
            subpixel.astype(f32),
            stretch_weight[..., None].astype(f32),
        ],
        axis=-1,
    )
    outer = outer_tables()
    outer_x = np.pad(outer.astype(np.float32), ((0, 0), (0, 112), (0, 0)))
    vm = pl.BlockSpec(memory_space=pltpu.VMEM)
    sm = pl.BlockSpec(memory_space=pltpu.SMEM)
    hbm = pl.BlockSpec(memory_space=pl.ANY)
    dma = pltpu.SemaphoreType.DMA
    recv, rfr, rsmall, moments, vmat = pl.pallas_call(
        warp_kernel,
        out_shape=(
            jax.ShapeDtypeStruct((NP, NS, ROWS, S), bf16),
            jax.ShapeDtypeStruct((NP, 16, S), bf16),
            jax.ShapeDtypeStruct((NP, 8, 384), f32),
            jax.ShapeDtypeStruct((16, 128), f32),
            jax.ShapeDtypeStruct((2, 512, 256), bf16),
        ),
        in_specs=[sm, sm, sm, hbm, vm, vm, vm, vm, vm],
        out_specs=(hbm, hbm, hbm, vm, vm),
        scratch_shapes=[
            pltpu.VMEM((NS, S, S), bf16),
            pltpu.VMEM((8, 256), f32),
            pltpu.VMEM((NS, S, S), bf16),
            pltpu.VMEM((16 * SPILL, S), bf16),
            pltpu.VMEM((896, S), bf16),
            pltpu.VMEM((S, S), bf16),
            pltpu.VMEM((S, S), bf16),
            pltpu.VMEM((NS, 128, S), bf16),
            pltpu.VMEM((2, 128, 256), bf16),
            pltpu.VMEM((8, 2 * S), f32),
            pltpu.VMEM((2, 16, S), f32),
            pltpu.VMEM((128, 384), f32),
            dma((NS,)), dma((NS,)), dma((NS,)),
            dma, dma, dma, dma,
        ],
        compiler_params=pltpu.CompilerParams(
            has_side_effects=True, vmem_limit_bytes=60 * 1024 * 1024, collective_id=1
        ),
        name="warp_send",
    )(params, route, tile, pix, row_mask, col_mask, psf_taps, outer, outer_x)

    codes = rsmall[:, :, 256].reshape(NP * NS).astype(jnp.int32)
    slab, spill, wmsg = pl.pallas_call(
        layer_kernel,
        out_shape=(
            jax.ShapeDtypeStruct((2, 64, ROWS, 256), bf16),
            jax.ShapeDtypeStruct((256, 256), bf16),
            jax.ShapeDtypeStruct((NV, 2 * NP, 768), bf16),
        ),
        in_specs=[sm, hbm, hbm, vm, vm],
        out_specs=(vm, vm, vm),
        scratch_shapes=[
            pltpu.VMEM((NP, NS, ROWS, S), bf16),
            pltpu.VMEM((2, 2, 66, ROWS, 256), f32),
            pltpu.VMEM((2, 66, 8, 256), f32),
            pltpu.VMEM((NP, 16, S), bf16),
            dma((4,)),
            dma,
        ],
        compiler_params=pltpu.CompilerParams(vmem_limit_bytes=60 * 1024 * 1024),
        name="layer_smooth",
    )(codes, recv, rfr, vmat, rsmall)

    pick_row = np.zeros((160, 16), np.float32)
    pick_col = np.zeros((160, 128), np.float32)
    for q in range(10):
        for r in range(10):
            pick_row[16 * q + r, 4 * PAIRS[q][0] + PAIRS[r][0]] = 1
            pick_col[16 * q + r, 4 * PAIRS[q][1] + PAIRS[r][1]] = 1
    flux, weight, hessian = pl.pallas_call(
        owner_kernel,
        out_shape=(
            jax.ShapeDtypeStruct((128, 2 * S), f32),
            jax.ShapeDtypeStruct((128, 2 * S), f32),
            jax.ShapeDtypeStruct((1, 10, 10), f32),
        ),
        in_specs=[hbm, hbm, hbm, hbm, vm, vm],
        out_specs=(vm, vm, vm),
        scratch_shapes=[
            pltpu.VMEM((2, 2, NV, 4, ROWS, 256), bf16),
            pltpu.VMEM((2, 8, ROWS, 256), bf16),
            pltpu.VMEM((4, 4, ROWS, 256), bf16),
            pltpu.VMEM((NV, 2 * NP, 768), bf16),
            pltpu.VMEM((NV, 32, 256), bf16),
            pltpu.VMEM((32, 256), bf16),
            pltpu.VMEM((SPILL, 32, 256), bf16),
            dma((2, 2)), dma((2, 2)), dma((2, 2)), dma, dma, dma,
            dma, dma, dma((2, 2)), dma,
            pltpu.VMEM((NV, 16, 128), f32),
            dma, dma,
        ],
        compiler_params=pltpu.CompilerParams(
            has_side_effects=True, vmem_limit_bytes=48 * 1024 * 1024, collective_id=2
        ),
        name="owner_sum",
    )(slab, spill, wmsg, moments, pick_row, pick_col)

    return flux, weight, hessian


def solution(mesh):
    in_specs = (
        P("patch", "visit", None, None, None),
        P("patch", "visit", None, None),
        P("patch", "visit", None, None),
        P("patch", "visit", None),
        P("patch", "visit", None),
        P("patch", "visit", None, None),
        P("patch", "visit", None, None),
        P("patch", "visit", None),
        P("patch", "visit", None),
        P("visit", None, None),
    )
    out_specs = (P("visit", "patch"), P("visit", "patch"), P("patch", None, None))
    return jax.shard_map(body, mesh=mesh, in_specs=in_specs, out_specs=out_specs, check_vma=False)
```
